256 devices in a mesh: row: 16 (over z_lo, x, core), col: 16 (over z_hi, y).
Axes of the slice: x: 4, y: 4, z: 8 (z_hi: 4, z_lo: 2; z = z_hi * 2 + z_lo), core: 2. Of those that a mesh axis runs over, the one named last changes fastest.
Arguments:
- tokens: bfloat16 [512, 8192], P('col', 'row'), may hold values from -6 to 6
- out_grad: bfloat16 [512, 8192], P('col', 'row'), may hold values from -6 to 6
- seq_ids: int32 [512], P('col'), may hold values from 0 to 7, never falling along the last dimension, each value on 1 to 128 neighbouring positions
- confidence: int32 [8], replicated, may hold values from 1 to 8
- gate_weight: bfloat16 [8192, 28672], P('row', 'col'), may hold values from -0.0625 to 0.0625
- up_weight: bfloat16 [8192, 28672], P('row', 'col'), may hold values from -0.0625 to 0.0625
- down_weight: bfloat16 [28672, 8192], P('col', 'row'), may hold values from -0.03125 to 0.03125
Outputs:
- grad_tokens: bfloat16 [512, 8192], P('col', 'row')
- grad_gate: bfloat16 [8192, 28672], P('row', 'col')
- grad_up: bfloat16 [8192, 28672], P('row', 'col')
- grad_down: bfloat16 [28672, 8192], P('col', 'row')
The draws below stay inside these ranges and needn't reach their ends.
Inputs may be any that keep to these rules, and one draw needn't show every extreme that they name: `seq_ids`: sequence numbers never fall along the tokens; each sequence has 1 to 128 tokens.
All inputs are finite; a program needn't handle non-finite values.
Results may differ from the reference program's by a relative error of at most 0.0054.
Values may be sent and summed in bfloat16 or wider, within the bound.
A program may use at most 128 MiB of HBM per device.

```python
import math
import jax
import jax.numpy as jnp
import numpy as np

D = 8192
FF = 28672
SEQS = 8
TOKENS = 512
SEQ_MOST = 128


def plant(entries, rng, low, top_value):
    longest = entries.shape.index(max(entries.shape))
    spots = []
    for shift in (0, 1):
        where = [jax.random.randint(jax.random.fold_in(rng, axis), (), 0, length) for axis, length in enumerate(entries.shape)]
        where[longest] = (where[longest] + shift) % entries.shape[longest]
        spots.append(tuple(where))
    return entries.at[spots[0]].set(low).at[spots[1]].set(top_value)


def shard_levels(own_key, extent, split, low, top_value):
    def one(position, shards_of):
        draws = jax.random.uniform(jax.random.fold_in(jax.random.fold_in(own_key, 6), position), (shards_of,), jnp.float32, low / len(split), top_value / len(split))
        return jnp.repeat(jnp.exp(draws), extent[position] // shards_of).reshape((-1,) + (1,) * (len(extent) - position - 1))

    loudness = one(*split[0])
    for cut in split[1:]:
        loudness = loudness * one(*cut)
    return loudness


def length_profile(count, total, bound, lean):
    portions = [(1 << 20) // math.isqrt(standing ** lean) + 1 for standing in range(2, count + 1)]
    surplus, holding = total - bound - (count - 1), [1] * (count - 1)
    while surplus > 0:
        movable = [i for i in range(count - 1) if holding[i] < bound]
        whole, budget = sum([portions[i] for i in movable]), surplus
        for i in movable:
            extra = min(bound - holding[i], max(1, budget * portions[i] // whole), surplus)
            holding[i] = holding[i] + extra
            surplus = surplus - extra
    return np.array([bound] + holding)


def uneven(stream_key, number_of, total, limit, slope):
    if number_of == 2:
        one = jax.random.randint(stream_key, (), max(1, total - limit), min(limit, total - 1) + 1)
        return jnp.stack([one, total - one])
    lengths = jnp.asarray(length_profile(number_of, total, limit, slope), jnp.int32)
    couples = (number_of - 1) // 2
    source_of, sink = lengths[1:1 + 2 * couples:2], lengths[2:2 + 2 * couples:2]
    room = jnp.minimum(source_of - 1, limit - sink)
    passed = jax.random.randint(jax.random.fold_in(stream_key, 1), (couples,), 0, 1 << 20) % (room + 1)
    lengths = lengths.at[1:1 + 2 * couples:2].set(source_of - passed).at[2:2 + 2 * couples:2].set(sink + passed)
    return lengths[jax.random.permutation(jax.random.fold_in(stream_key, 2), number_of)]


def gaussian(own_key, extent, scale, reach, shards=(), held_as=jnp.bfloat16):
    array = scale * jax.random.normal(own_key, extent, jnp.float32)
    if shards:
        array = array * shard_levels(own_key, extent, shards, -0.22, 0.18)
    return jnp.clip(array, -reach, reach).astype(held_as)


def setup_inputs(seed: int = 0) -> dict:
    streams_of = jax.random.split(jax.random.key(seed), 8)
    return {
        "tokens": gaussian(streams_of[0], (TOKENS, D), 1.0, 6.0, ((0, 16), (1, 16))),
        "out_grad": gaussian(streams_of[1], (TOKENS, D), 1.0, 6.0, ((0, 16), (1, 16))),
        "seq_ids": jnp.searchsorted(jnp.cumsum(uneven(streams_of[2], SEQS, TOKENS, SEQ_MOST, 0)), jnp.arange(TOKENS), side="right").astype(jnp.int32),
        "confidence": plant(jax.random.randint(streams_of[3], (SEQS,), 1, 9), jax.random.fold_in(streams_of[3], 1), 1, 8).astype(jnp.int32),
        "gate_weight": gaussian(streams_of[4], (D, FF), D ** -0.5, 0.0625, ((0, 16), (1, 16))),
        "up_weight": gaussian(streams_of[5], (D, FF), D ** -0.5, 0.0625, ((0, 16), (1, 16))),
        "down_weight": gaussian(streams_of[6], (FF, D), FF ** -0.5, 0.03125, ((0, 16), (1, 16))),
    }


def reference(tokens, out_grad, seq_ids, confidence, gate_weight, up_weight, down_weight):
    factor = confidence[seq_ids].astype(jnp.float32) / 4.0
    weighted = (out_grad.astype(jnp.float32) * factor[:, None]).astype(jnp.bfloat16)
    gate = jnp.dot(tokens, gate_weight, preferred_element_type=jnp.float32)
    up = jnp.dot(tokens, up_weight, preferred_element_type=jnp.float32)
    grad_hidden = jnp.dot(weighted, down_weight.T, preferred_element_type=jnp.float32)
    sig = jax.nn.sigmoid(gate)
    silu_gate = gate * sig
    hidden = (silu_gate * up).astype(jnp.bfloat16)
    grad_pre_gate = (grad_hidden * up * sig * (1.0 + gate * (1.0 - sig))).astype(jnp.bfloat16)
    grad_pre_up = (grad_hidden * silu_gate).astype(jnp.bfloat16)
    grad_down = jnp.dot(hidden.T, weighted, preferred_element_type=jnp.float32).astype(jnp.bfloat16)
    grad_gate = jnp.dot(tokens.T, grad_pre_gate, preferred_element_type=jnp.float32).astype(jnp.bfloat16)
    grad_up = jnp.dot(tokens.T, grad_pre_up, preferred_element_type=jnp.float32).astype(jnp.bfloat16)
    grad_tokens = jnp.dot(grad_pre_gate, gate_weight.T, preferred_element_type=jnp.float32)
    grad_tokens = grad_tokens + jnp.dot(grad_pre_up, up_weight.T, preferred_element_type=jnp.float32)
    return grad_tokens.astype(jnp.bfloat16), grad_gate, grad_up, grad_down
```

```python
import functools

import jax
import jax.numpy as jnp
from jax import lax
from jax.experimental import pallas as pl
from jax.experimental.pallas import tpu as pltpu
from jax.sharding import PartitionSpec as P

MESH = pl.DeviceIdType.MESH
BF16, F32 = jnp.bfloat16, jnp.float32
NX, NZ, NH, NY = 4, 2, 4, 4
ORDER = (0, 1, 3, 2)
CHUNKS = 4
GX = 9


def contract_last(left, right):
    return lax.dot_general(left, right, (((1,), (1,)), ((), ())), preferred_element_type=F32)


def contract_first(left, right):
    return lax.dot_general(left, right, (((0,), (0,)), ((), ())), preferred_element_type=F32)


def main_kernel(
    seq_ref, conf_ref, tok_ref, og_ref, gate_hbm, up_hbm, down_hbm,
    gtok_ref, h_hbm, a_hbm,
    acts, wg, wu, wd, wg2, wu2,
    part, rx1, rz1, rx2, rz2, own, sx2, sz2, tot, hb, hs,
    gt, sd, rd, se, re, st,
    lsem, wsend, wrecv, asend, arecv, ysend, yrecv, csend, crecv,
    x1s, x1r, z1s, z1r, x2s, x2r, z2s, z2r,
    ax1s, ax1r, az1s, az1r, ax2s, ax2r, az2s, az2r,
    hss, hsr, ds_, dr_, es_, er_,
):
    row, col = lax.axis_index("row"), lax.axis_index("col")
    z, x, c = row // 8, (row // 2) % 4, row % 2
    zh, y = col // 4, col % 4
    sib = 1 - c
    width = wg.shape[2]
    groups = width // 128
    total = 3 * groups

    def dev(x=x, z=z, c=c, zh=zh, y=y):
        return (z * 8 + x * 2 + c, zh * 4 + y)

    def xpeer(i):
        return dev(x=(x + i) % NX)

    def ypeer(i):
        return dev(y=(y + i) % NY)

    def hpeer(i):
        return dev(zh=(zh + i) % NH)

    zpeer, speer = dev(z=1 - z), dev(c=sib)

    def remote(src, dst, ssem, rsem, peer):
        return pltpu.make_async_remote_copy(
            src_ref=src, dst_ref=dst, send_sem=ssem, recv_sem=rsem,
            device_id=peer, device_id_type=MESH,
        )

    sent = []

    def start(copy):
        copy.start()
        sent.append(copy)
        return copy

    bar = pltpu.get_barrier_semaphore()
    peers = [xpeer(i) for i in (1, 2, 3)] + [ypeer(i) for i in (1, 2, 3)]
    peers += [hpeer(i) for i in (1, 2, 3)] + [zpeer, speer]
    for peer in peers:
        pl.semaphore_signal(bar, inc=1, device_id=peer, device_id_type=MESH)

    mine = pl.ds(pl.multiple_of(c * width, 128), width)
    theirs = pl.ds(pl.multiple_of(sib * width, 128), width)
    loads = [
        pltpu.make_async_copy(gate_hbm.at[:, mine], wg.at[c], lsem.at[0]),
        pltpu.make_async_copy(up_hbm.at[:, mine], wu.at[c], lsem.at[1]),
        pltpu.make_async_copy(down_hbm.at[mine, :], wd.at[c], lsem.at[2]),
        pltpu.make_async_copy(gate_hbm.at[:, theirs], wg2, lsem.at[3]),
        pltpu.make_async_copy(up_hbm.at[:, theirs], wu2, lsem.at[4]),
    ]
    for copy in loads:
        copy.start()

    rows = tok_ref.shape[0]
    at = lax.broadcasted_iota(jnp.int32, (rows, 1), 0)
    factor = jnp.zeros((rows, 1), F32)
    for i in range(rows):
        factor = jnp.where(at == i, conf_ref[seq_ref[i]].astype(F32) * 0.25, factor)
    here = pl.ds(pl.multiple_of(zh * rows, rows), rows)
    acts[c, y, 0, here, :] = tok_ref[...]
    acts[c, y, 1, here, :] = (og_ref[...].astype(F32) * factor).astype(BF16)

    pl.semaphore_wait(bar, len(peers))

    block = acts.at[c, y, :, here, :]
    gather = [
        start(remote(block, block, asend.at[i - 1], arecv.at[i - 1], hpeer(i))) for i in (1, 3, 2)
    ]
    weights = [
        start(remote(gate_hbm.at[:, theirs], wg.at[c], wsend.at[0], wrecv.at[0], speer)),
        start(remote(up_hbm.at[:, theirs], wu.at[c], wsend.at[1], wrecv.at[1], speer)),
        start(remote(down_hbm.at[theirs, :], wd.at[c], wsend.at[2], wrecv.at[2], speer)),
    ]
    for copy in gather:
        copy.wait_recv()
    plane = acts.at[c, y]
    cross = {0: start(remote(plane, plane, csend.at[0], crecv.at[0], speer))}
    gather_y = {
        i: start(remote(plane, plane, ysend.at[i - 1], yrecv.at[i - 1], ypeer(i))) for i in (1, 3, 2)
    }
    keep = []

    def forward(k):
        chunk = (y + ORDER[k]) % NY
        if k == 0:
            for copy in loads:
                copy.wait()
        cross[k].wait_recv()
        if k == 0:
            for copy in weights:
                copy.wait_recv()

        def put(first, value):
            for g in range(groups):
                part[k, :, :, first + g] = (
                    value[:, g * 128 : (g + 1) * 128].astype(BF16).reshape(NX, NZ, 16, 128)
                )

        t0, t1 = acts[0, chunk, 0], acts[1, chunk, 0]
        put(0, jnp.dot(t0, wg[0], preferred_element_type=F32)
            + jnp.dot(t1, wg[1], preferred_element_type=F32))
        put(groups, jnp.dot(t0, wu[0], preferred_element_type=F32)
            + jnp.dot(t1, wu[1], preferred_element_type=F32))
        step = {}
        for i in (1, 3, 2):
            step["x", i] = start(remote(
                part.at[k, (x + i) % NX, :, pl.ds(0, GX)], rx1.at[k, i - 1],
                x1s.at[k, i - 1], x1r.at[k, i - 1], xpeer(i)))
        put(2 * groups, contract_last(acts[0, chunk, 1], wd[0])
            + contract_last(acts[1, chunk, 1], wd[1]))
        step["z"] = start(remote(
            part.at[k, :, 1 - z, pl.ds(GX, total - GX)], rz1.at[k], z1s.at[k], z1r.at[k], zpeer))
        return step

    def second(k, step):
        after = {}
        step["z"].wait_recv()
        for i in (0, 1, 2, 3):
            dest = (x + i) % NX
            value = part[k, dest, z, GX:].astype(F32) + rz1[k, dest].astype(F32)
            if i == 0:
                own[k, GX:] = value
            else:
                sz2[k, i - 1] = value.astype(BF16)
                after["x", i] = start(remote(
                    sz2.at[k, i - 1], rz2.at[k, i - 1], z2s.at[k, i - 1], z2r.at[k, i - 1], xpeer(i)))
        for i in (1, 3, 2):
            step["x", i].wait_recv()

        def summed(zz):
            value = part[k, x, zz, :GX].astype(F32)
            for i in range(3):
                value = value + rx1[k, i, zz].astype(F32)
            return value

        sx2[k] = summed(1 - z).astype(BF16)
        after["z"] = start(remote(sx2.at[k], rx2.at[k], x2s.at[k], x2r.at[k], zpeer))
        own[k, :GX] = summed(z)
        return after

    def pointwise(k, step):
        step["z"].wait_recv()
        tot[:GX] = own[k, :GX] + rx2[k].astype(F32)
        for i in (1, 3, 2):
            step["x", i].wait_recv()
        value = own[k, GX:]
        for i in range(3):
            value = value + rz2[k, i].astype(F32)
        tot[GX:] = value
        gate, up, gh = tot[:groups], tot[groups : 2 * groups], tot[2 * groups :]
        sig = 1.0 / (1.0 + jnp.exp(-gate))
        silu = gate * sig
        hb[k, x, z, :groups] = (silu * up).astype(BF16)
        hb[k, x, z, groups : 2 * groups] = (gh * up * sig * (1.0 + gate * (1.0 - sig))).astype(BF16)
        hb[k, x, z, 2 * groups :] = (gh * silu).astype(BF16)
        after = {}
        head, tail = hb.at[k, x, z, pl.ds(0, GX)], hb.at[k, x, z, pl.ds(GX, total - GX)]
        after["z"] = start(remote(head, head, az1s.at[k], az1r.at[k], zpeer))
        for i in (1, 3, 2):
            after["x", i] = start(
                remote(tail, tail, ax1s.at[k, i - 1], ax1r.at[k, i - 1], xpeer(i)))
        return after

    def spread(k, step):
        after = {}
        step["z"].wait_recv()
        head = hb.at[k, x, :, pl.ds(0, GX)]
        for i in (1, 3, 2):
            after["x", i] = start(
                remote(head, head, ax2s.at[k, i - 1], ax2r.at[k, i - 1], xpeer(i)))
        for i in (1, 3, 2):
            step["x", i].wait_recv()
        tail = hb.at[k, :, z, pl.ds(GX, total - GX)]
        after["z"] = start(remote(tail, tail, az2s.at[k], az2r.at[k], zpeer))
        return after

    def share(k, step):
        for i in (1, 3, 2):
            step["x", i].wait_recv()
        step["z"].wait_recv()
        chunk = (y + ORDER[k]) % NY
        copy = pltpu.make_async_copy(hb.at[k], h_hbm.at[c, chunk], lsem.at[5 + 2 * k])
        copy.start()
        keep.append(copy)
        return start(remote(hb.at[k], hs.at[k], hss.at[k], hsr.at[k], speer))

    def backward(k, copy):
        def flat(ref, first):
            return jnp.concatenate(
                [ref[k, :, :, first + g].reshape(NX * NZ * 16, 128) for g in range(groups)], axis=1)

        value = contract_last(flat(hb, groups), wg[c]) + contract_last(flat(hb, 2 * groups), wu[c])
        copy.wait_recv()
        chunk = (y + ORDER[k]) % NY
        out = pltpu.make_async_copy(hs.at[k], h_hbm.at[sib, chunk], lsem.at[6 + 2 * k])
        out.start()
        keep.append(out)
        value = value + contract_last(flat(hs, groups), wg2[...]) + contract_last(flat(hs, 2 * groups), wu2[...])
        i = ORDER[k]
        if i == 0:
            gt[...] = value
            return None
        sd[i - 1] = value.astype(BF16)
        return start(remote(sd.at[i - 1], rd.at[i - 1], ds_.at[i - 1], dr_.at[i - 1], ypeer(i)))

    def take(k):
        i = (NY - ORDER[k]) % NY
        gather_y[i].wait_recv()
        got = acts.at[c, (y + ORDER[k]) % NY]
        cross[k] = start(remote(got, got, csend.at[k], crecv.at[k], speer))

    s1, s2, s3, s4, s5, s6 = {}, {}, {}, {}, {}, {}
    s1[0] = forward(0)
    take(1)
    take(2)
    s1[1] = forward(1)
    s2[0] = second(0, s1[0])
    s3[0] = pointwise(0, s2[0])
    s1[2] = forward(2)
    take(3)
    s2[1] = second(1, s1[1])
    s4[0] = spread(0, s3[0])
    s3[1] = pointwise(1, s2[1])
    s5[0] = share(0, s4[0])
    s1[3] = forward(3)
    s2[2] = second(2, s1[2])
    s4[1] = spread(1, s3[1])
    s6[0] = backward(0, s5[0])
    s3[2] = pointwise(2, s2[2])
    s5[1] = share(1, s4[1])
    s2[3] = second(3, s1[3])
    s4[2] = spread(2, s3[2])
    s6[1] = backward(1, s5[1])
    s3[3] = pointwise(3, s2[3])
    s5[2] = share(2, s4[2])
    s4[3] = spread(3, s3[3])
    s6[2] = backward(2, s5[2])
    s5[3] = share(3, s4[3])
    s6[3] = backward(3, s5[3])
    out = pltpu.make_async_copy(acts.at[c], a_hbm, lsem.at[13])
    out.start()
    keep.append(out)

    for k in range(1, CHUNKS):
        s6[k].wait_recv()
    value = gt[...]
    for i in range(3):
        value = value + rd[i].astype(F32)
    st[...] = value
    last = {}
    for i in (2, 1, 3):
        there = pl.ds(pl.multiple_of(((zh + i) % NH) * rows, rows), rows)
        se[i - 1] = st[there, :].astype(BF16)
        last[i] = start(remote(se.at[i - 1], re.at[i - 1], es_.at[i - 1], er_.at[i - 1], hpeer(i)))
    value = st[here, :]
    for i in (1, 3, 2):
        last[i].wait_recv()
        value = value + re[i - 1].astype(F32)
    gtok_ref[...] = value.astype(BF16)
    for copy in sent:
        copy.wait_send()
    for copy in keep:
        copy.wait()


def grads_kernel(a_hbm, h_hbm, gg_hbm, gu_hbm, gd_hbm, acts, h, og, ou, od, lsem, osem):
    chunks, _, _, total = h_hbm.shape[1:5]
    groups = total // 3
    width = groups * 128
    loads = [pltpu.make_async_copy(a_hbm, acts, lsem.at[0])]
    loads[0].start()
    order = [(half, which) for half in range(2) for which in (1, 2, 0)]
    for n, (half, which) in enumerate(order):
        span = pl.ds(which * groups, groups)
        copy = pltpu.make_async_copy(
            h_hbm.at[half, :, :, :, span], h.at[half, :, :, :, span], lsem.at[n + 1])
        copy.start()
        loads.append(copy)
    loads[0].wait()
    tokens, depth = chunks * acts.shape[2], acts.shape[3]
    stores = []
    for n, (half, which) in enumerate(order):
        loads[n + 1].wait()
        right = jnp.concatenate(
            [h[half, :, :, :, which * groups + g].reshape(tokens, 128) for g in range(groups)], axis=1)
        left = acts[:, 1 if which == 0 else 0].reshape(tokens, depth)
        span = pl.ds(half * width, width)
        if which == 0:
            od[span, :] = contract_first(right, left).astype(BF16)
            copy = pltpu.make_async_copy(od.at[span, :], gd_hbm.at[span, :], osem.at[n])
        else:
            ref, hbm = ((og, gg_hbm), (ou, gu_hbm))[which - 1]
            ref[:, span] = contract_first(left, right).astype(BF16)
            copy = pltpu.make_async_copy(ref.at[:, span], hbm.at[:, span], osem.at[n])
        copy.start()
        stores.append(copy)
    for copy in stores:
        copy.wait()


def local(tokens, out_grad, seq_ids, confidence, gate_weight, up_weight, down_weight):
    rows, depth = tokens.shape
    width = gate_weight.shape[1] // 2
    groups = width // 128
    total = 3 * groups
    gz = total - GX
    chunk = rows * NH
    vm, dma = pltpu.VMEM, pltpu.SemaphoreType.DMA
    anyspace = pl.BlockSpec(memory_space=pl.ANY)
    vmspace = pl.BlockSpec(memory_space=pltpu.VMEM)
    smspace = pl.BlockSpec(memory_space=pltpu.SMEM)
    four, three = (CHUNKS,), (CHUNKS, 3)
    grad_tokens, h, acts = pl.pallas_call(
        main_kernel,
        name="exchange",
        out_shape=(
            jax.ShapeDtypeStruct((rows, depth), BF16),
            jax.ShapeDtypeStruct((2, NY, NX, NZ, total, 16, 128), BF16),
            jax.ShapeDtypeStruct((NY, 2, chunk, depth), BF16),
        ),
        in_specs=[smspace, smspace, vmspace, vmspace, anyspace, anyspace, anyspace],
        out_specs=(vmspace, anyspace, anyspace),
        scratch_shapes=[
            vm((2, NY, 2, chunk, depth), BF16),
            vm((2, depth, width), BF16),
            vm((2, depth, width), BF16),
            vm((2, width, depth), BF16),
            vm((depth, width), BF16),
            vm((depth, width), BF16),
            vm((CHUNKS, NX, NZ, total, 16, 128), BF16),
            vm((CHUNKS, 3, NZ, GX, 16, 128), BF16),
            vm((CHUNKS, NX, gz, 16, 128), BF16),
            vm((CHUNKS, GX, 16, 128), BF16),
            vm((CHUNKS, 3, gz, 16, 128), BF16),
            vm((CHUNKS, total, 16, 128), F32),
            vm((CHUNKS, GX, 16, 128), BF16),
            vm((CHUNKS, 3, gz, 16, 128), BF16),
            vm((total, 16, 128), F32),
            vm((CHUNKS, NX, NZ, total, 16, 128), BF16),
            vm((CHUNKS, NX, NZ, total, 16, 128), BF16),
            vm((chunk, depth), F32),
            vm((3, chunk, depth), BF16),
            vm((3, chunk, depth), BF16),
            vm((3, rows, depth), BF16),
            vm((3, rows, depth), BF16),
            vm((chunk, depth), F32),
            dma((14,)), dma((3,)), dma((3,)), dma((3,)), dma((3,)), dma((3,)), dma((3,)),
            dma(four), dma(four),
            dma(three), dma(three), dma(four), dma(four), dma(four), dma(four), dma(three), dma(three),
            dma(three), dma(three), dma(four), dma(four), dma(three), dma(three), dma(four), dma(four),
            dma(four), dma(four), dma((3,)), dma((3,)), dma((3,)), dma((3,)),
        ],
        compiler_params=pltpu.CompilerParams(
            collective_id=0, has_side_effects=True, vmem_limit_bytes=48 << 20),
    )(seq_ids, confidence, tokens, out_grad, gate_weight, up_weight, down_weight)
    grad_gate, grad_up, grad_down = pl.pallas_call(
        grads_kernel,
        name="weight_grads",
        out_shape=(
            jax.ShapeDtypeStruct((depth, 2 * width), BF16),
            jax.ShapeDtypeStruct((depth, 2 * width), BF16),
            jax.ShapeDtypeStruct((2 * width, depth), BF16),
        ),
        in_specs=[anyspace, anyspace],
        out_specs=(anyspace, anyspace, anyspace),
        scratch_shapes=[
            vm((NY, 2, chunk, depth), BF16),
            vm((2, NY, NX, NZ, total, 16, 128), BF16),
            vm((depth, 2 * width), BF16),
            vm((depth, 2 * width), BF16),
            vm((2 * width, depth), BF16),
            dma((7,)),
            dma((6,)),
        ],
        compiler_params=pltpu.CompilerParams(vmem_limit_bytes=48 << 20),
    )(acts, h)
    return grad_tokens, grad_gate, grad_up, grad_down


def solution(mesh):
    placed = (
        P("col", "row"),
        P("col", "row"),
        P("col"),
        P(),
        P("row", "col"),
        P("row", "col"),
        P("col", "row"),
    )
    return jax.shard_map(
        local,
        mesh=mesh,
        in_specs=placed,
        out_specs=(P("col", "row"), P("row", "col"), P("row", "col"), P("col", "row")),
        check_vma=False,
    )
```

```python
import jax
import jax.numpy as jnp
from jax import lax
from jax.experimental import pallas as pl
from jax.experimental.pallas import tpu as pltpu
from jax.sharding import PartitionSpec as P

MESH = pl.DeviceIdType.MESH
BF16, F32 = jnp.bfloat16, jnp.float32
NX, NZ, NH, NY = 4, 2, 4, 4
CHUNKS = 4
ORDER = (0, 1, 3, 2)
NA = 5
SCHEDULE = (
    "T0", "Z2", "FA0", "FB0", "Z1", "Z3", "MA0", "T2", "SB0", "FA2", "FB2", "T1", "SA0", "MB0", "FA1", "FB1",
    "T3", "MA2", "SB2", "FA3", "PB0", "FB3", "PA0", "MA1", "SB1", "SA2", "MB2", "SB3", "MA3", "AA0", "WB0",
    "PA2", "SA1", "MB1", "PB2", "MB3", "SA3", "AA2", "PA1", "WA0", "YB0", "PB1", "WB2", "PA3", "PB3", "AA1",
    "WA2", "HB0", "HA0", "BA0", "BB0", "YB2", "WB1", "AA3", "WB3", "C0", "WA1", "HB2", "HA2", "BA2", "BB2",
    "YB1", "D0", "C2", "WA3", "YB3", "HA1", "BA1", "HB1", "BB1", "HA3", "BA3", "D2", "C1", "HB3", "BB3",
    "G0", "G1", "C3", "G2", "G3", "G4", "D1", "G5", "D3", "E0",
)

def contract_last(left, right):
    return lax.dot_general(left, right, (((1,), (1,)), ((), ())), preferred_element_type=F32)


def contract_first(left, right):
    return lax.dot_general(left, right, (((0,), (0,)), ((), ())), preferred_element_type=F32)


def pointwise(gate, up, gh):
    sig = 1.0 / (1.0 + jnp.exp(-gate))
    silu = gate * sig
    hidden = (silu * up).astype(BF16)
    grad_pre_gate = (gh * up * sig * (1.0 + gate * (1.0 - sig))).astype(BF16)
    grad_pre_up = (gh * silu).astype(BF16)
    return hidden, grad_pre_gate, grad_pre_up


def main_kernel(
    seq_hbm, conf_hbm, tok_hbm, grad_hbm, gate_hbm, up_hbm, down_hbm,
    gtok_ref, gg_hbm, gu_hbm, gd_hbm,
    seq, conf, raw, acts, wg, wu, wd, part, full,
    far_a, fin_a, sum_a, mid_a, out_a, in_a, own_a,
    in_b, full_b, part_b, far_b, fin_b, sum_b, mid_b,
    tot, hb, hs, gp, gq, gr, sd, rd, se, re, own_t, og, ou, od,
    lsem, osem, wsem, hsem, ysem, csem,
    far_as, fin_as, sum_as, z_as, gz_as, gx_as, gw_as, sh_as,
    far_bs, fin_bs, sum_bs, z_bs, gz_bs, gx_bs, gw_bs, sh_bs,
    psem, dsem, esem,
):
    row, col = lax.axis_index("row"), lax.axis_index("col")
    z, x, c = row // 8, (row // 2) % 4, row % 2
    zh, y = col // 4, col % 4
    sib = 1 - c
    width = wg.shape[2]
    groups = width // 128
    nb = groups - NA
    ga, gb = 3 * NA, 3 * nb
    rows = raw.shape[0]
    right, left = (x + 1) % NX, (x + 3) % NX
    across = (x + 2) % NX

    def dev(x=x, z=z, c=c, zh=zh, y=y):
        return (z * 8 + x * 2 + c, zh * 4 + y)

    def ypeer(i):
        return dev(y=(y + i) % NY)

    def hpeer(i):
        return dev(zh=(zh + i) % NH)

    zpeer, speer = dev(z=1 - z), dev(c=sib)
    xpeers = (dev(x=right), dev(x=left))

    sent, kept, state = [], [], {}

    def send(key, src, dst, sems, index, peer):
        copy = pltpu.make_async_remote_copy(
            src_ref=src, dst_ref=dst, send_sem=sems.at[(0,) + index], recv_sem=sems.at[(1,) + index],
            device_id=peer, device_id_type=MESH)
        copy.start()
        sent.append(copy)
        state[key] = copy

    def wait(key):
        state[key].wait_recv()

    def local(src, dst, sem):
        copy = pltpu.make_async_copy(src, dst, sem)
        copy.start()
        return copy

    bar = pltpu.get_barrier_semaphore()
    peers = list(xpeers) + [ypeer(i) for i in (1, 2, 3)] + [hpeer(i) for i in (1, 2, 3)] + [zpeer, speer]
    for peer in peers:
        pl.semaphore_signal(bar, inc=1, device_id=peer, device_id_type=MESH)

    def yrows(i):
        return pl.ds(pl.multiple_of(((y + i) % NY) * rows, rows), rows)

    first = [
        local(seq_hbm, seq, lsem.at[0]),
        local(conf_hbm, conf, lsem.at[1]),
        local(grad_hbm, raw, lsem.at[2]),
        local(tok_hbm, acts.at[c, zh, 0, yrows(0), :], lsem.at[3]),
    ]
    mine = pl.ds(pl.multiple_of(c * width, 128), width)
    theirs = pl.ds(pl.multiple_of(sib * width, 128), width)
    loads = [
        local(gate_hbm.at[:, mine], wg.at[c], lsem.at[4]),
        local(up_hbm.at[:, mine], wu.at[c], lsem.at[5]),
        local(down_hbm.at[mine, :], wd.at[c], lsem.at[6]),
    ]
    for copy in first:
        copy.wait()
    at = lax.broadcasted_iota(jnp.int32, (rows, 1), 0)
    factor = jnp.zeros((rows, 1), F32)
    for i in range(rows):
        factor = jnp.where(at == i, conf[seq[i]].astype(F32) * 0.25, factor)
    acts[c, zh, 1, yrows(0), :] = (raw[...].astype(F32) * factor).astype(BF16)
    pl.semaphore_wait(bar, len(peers))

    def plane(k):
        return (zh + ORDER[k]) % NH

    def to_y(k):
        block = acts.at[c, plane(k), :, yrows(0), :]
        for i in (1, 3, 2):
            send(("y", k, i), block, block, ysem, (k, i - 1), ypeer(i))

    to_y(0)
    block = acts.at[c, zh, :, yrows(0), :]
    for i in (1, 3, 2):
        send(("h", i), block, block, hsem, (i - 1,), hpeer(i))
    send(("w", 0), gate_hbm.at[:, theirs], wg.at[c], wsem, (0,), speer)
    send(("w", 1), up_hbm.at[:, theirs], wu.at[c], wsem, (1,), speer)
    send(("w", 2), down_hbm.at[theirs, :], wd.at[c], wsem, (2,), speer)

    def pass_y(k):
        wait(("h", (NH - ORDER[k]) % NH))
        to_y(k)

    def take(k):
        for i in (1, 3, 2):
            wait(("y", k, i))
        got = acts.at[c, plane(k)]
        send(("c", k), got, got, csem, (k,), speer)

    def product(k, which, lo, n):
        span = pl.ds(lo * 128, n * 128)
        arr = 1 if which == 2 else 0
        t0, t1 = acts[0, plane(k), arr], acts[1, plane(k), arr]
        if which == 2:
            value = contract_last(t0, wd[0, span, :]) + contract_last(t1, wd[1, span, :])
        else:
            w = (wg, wu)[which]
            value = jnp.dot(t0, w[0, :, span], preferred_element_type=F32) + jnp.dot(
                t1, w[1, :, span], preferred_element_type=F32)
        base = which * NA if lo == 0 else ga + which * nb
        for g in range(n):
            v = value[:, g * 128 : (g + 1) * 128].reshape(NX, NZ, 16, 128)
            full[k, :, :, base + g] = v
            part[k, :, :, base + g] = v.astype(BF16)

    def halves(n, k):
        cut = (n + 1 - k % 2) // 2
        return (0, cut), (cut, n - cut)

    def forward_a(k):
        if k == 0:
            for copy in loads:
                copy.wait()
        wait(("c", k))
        for which in range(3):
            if k == 0:
                wait(("w", which))
            product(k, which, 0, NA)
        for d in range(2):
            lo, n = halves(ga, k)[d]
            send(("far_a", k, d), part.at[k, across, :, pl.ds(lo, n)], far_a.at[k, d, :, pl.ds(0, n)],
                 far_as, (k, d), xpeers[d])
        for d in range(2):
            lo, n = halves(ga, k)[1 - d]
            send(("fin_a", k, d), part.at[k, (right, left)[d], :, pl.ds(lo, n)],
                 fin_a.at[k, d, :, pl.ds(0, n)], fin_as, (k, d), xpeers[d])

    def middle_a(k):
        for d in range(2):
            lo, n = halves(ga, k)[d]
            wait(("far_a", k, d))
            value = full[k, (right, left)[d], :, lo : lo + n] + far_a[k, d, :, :n].astype(F32)
            mid_a[k, d, :, :n] = value.astype(BF16)
            span = pl.ds(0, n)
            send(("sum_a", k, d), mid_a.at[k, d, :, span], sum_a.at[k, d, :, span],
                 sum_as, (k, d), xpeers[d])

    def second_a(k):
        for d in range(2):
            wait(("fin_a", k, d))
        for d in range(2):
            wait(("sum_a", k, d))
        for zz in (1 - z, z):
            for d in range(2):
                lo, n = halves(ga, k)[d]
                value = (full[k, x, zz, lo : lo + n] + sum_a[k, d, zz, :n].astype(F32)
                         + fin_a[k, 1 - d, zz, :n].astype(F32))
                if zz is z:
                    own_a[k, lo : lo + n] = value
                else:
                    out_a[k, lo : lo + n] = value.astype(BF16)
            if zz is not z:
                send(("z_a", k), out_a.at[k], in_a.at[k], z_as, (k,), zpeer)

    def point_a(k):
        wait(("z_a", k))
        value = own_a[k] + in_a[k].astype(F32)
        results = pointwise(value[:NA], value[NA : 2 * NA], value[2 * NA :])
        for which in range(3):
            hb[k, x, z, which * NA : (which + 1) * NA] = results[which]
        block = hb.at[k, x, z, pl.ds(0, ga)]
        send(("gz_a", k), block, block, gz_as, (k,), zpeer)

    def across_a(k):
        wait(("gz_a", k))
        block = hb.at[k, x, :, pl.ds(0, ga)]
        for d in range(2):
            send(("gx_a", k, d), block, block, gx_as, (k, d), xpeers[d])

    def onward_a(k):
        for d in range(2):
            lo, n = halves(ga, k)[d]
            wait(("gx_a", k, d))
            block = hb.at[k, (left, right)[d], :, pl.ds(lo, n)]
            send(("gw_a", k, d), block, block, gw_as, (k, d), xpeers[d])

    def share_a(k):
        for d in range(2):
            wait(("gw_a", k, d))
        send(("sh_a", k), hb.at[k, :, :, pl.ds(0, ga)], hs.at[k, :, :, pl.ds(0, ga)], sh_as, (k,), speer)

    def forward_b(k):
        for which in range(3):
            product(k, which, NA, nb)
        send(("z_b", k), part.at[k, :, 1 - z, pl.ds(ga, gb)], in_b.at[k], z_bs, (k,), zpeer)

    def second_b(k):
        wait(("z_b", k))
        value = full[k, :, z, ga:] + in_b[k].astype(F32)
        full_b[k] = value
        part_b[k] = value.astype(BF16)
        for d in range(2):
            lo, n = halves(gb, k)[d]
            send(("far_b", k, d), part_b.at[k, across, pl.ds(lo, n)], far_b.at[k, d, pl.ds(0, n)],
                 far_bs, (k, d), xpeers[d])
        for d in range(2):
            lo, n = halves(gb, k)[1 - d]
            send(("fin_b", k, d), part_b.at[k, (right, left)[d], pl.ds(lo, n)],
                 fin_b.at[k, d, pl.ds(0, n)], fin_bs, (k, d), xpeers[d])

    def middle_b(k):
        for d in range(2):
            lo, n = halves(gb, k)[d]
            wait(("far_b", k, d))
            value = full_b[k, (right, left)[d], lo : lo + n] + far_b[k, d, :n].astype(F32)
            mid_b[k, d, :n] = value.astype(BF16)
            span = pl.ds(0, n)
            send(("sum_b", k, d), mid_b.at[k, d, span], sum_b.at[k, d, span], sum_bs, (k, d), xpeers[d])

    def point_b(k):
        for d in range(2):
            wait(("fin_b", k, d))
        for d in range(2):
            wait(("sum_b", k, d))
        for d in range(2):
            lo, n = halves(gb, k)[d]
            tot[lo : lo + n] = (full_b[k, x, lo : lo + n] + sum_b[k, d, :n].astype(F32)
                                + fin_b[k, 1 - d, :n].astype(F32))
        results = pointwise(tot[:nb], tot[nb : 2 * nb], tot[2 * nb :])
        for which in range(3):
            hb[k, x, z, ga + which * nb : ga + (which + 1) * nb] = results[which]
        block = hb.at[k, x, z, pl.ds(ga, gb)]
        for d in range(2):
            send(("gx_b", k, d), block, block, gx_bs, (k, d), xpeers[d])

    def onward_b(k):
        for d in range(2):
            lo, n = halves(gb, k)[d]
            wait(("gx_b", k, d))
            block = hb.at[k, (left, right)[d], z, pl.ds(ga + lo, n)]
            send(("gw_b", k, d), block, block, gw_bs, (k, d), xpeers[d])

    def across_b(k):
        for d in range(2):
            wait(("gw_b", k, d))
        block = hb.at[k, :, z, pl.ds(ga, gb)]
        send(("gz_b", k), block, block, gz_bs, (k,), zpeer)

    def share_b(k):
        wait(("gz_b", k))
        send(("sh_b", k), hb.at[k, :, :, pl.ds(ga, gb)], hs.at[k, :, :, pl.ds(ga, gb)], sh_bs, (k,), speer)

    def flat(ref, k, first, n):
        return [ref[k, :, :, first + g].reshape(NX * NZ * 16, 128) for g in range(n)]

    def back(k, base, lo, n):
        dg = jnp.concatenate(flat(hb, k, base + n, n), axis=1)
        du = jnp.concatenate(flat(hb, k, base + 2 * n, n), axis=1)
        span = pl.ds(lo * 128, n * 128)
        return [contract_last(dg, wg[h, :, span]) + contract_last(du, wu[h, :, span]) for h in (sib, c)]

    def back_a(k):
        gq[k], gp[k] = back(k, 0, 0, NA)

    def back_b(k):
        other, own = back(k, ga, NA, nb)
        gq[k] = gq[k] + other
        send(("p", k), gq.at[k], gr.at[k], psem, (k,), speer)
        gp[k] = gp[k] + own

    def cols_send(k):
        wait(("p", k))
        gp[k] = gp[k] + gr[k]
        for i in (2, 1, 3):
            sd[k, i - 1] = gp[k, yrows(i), :].astype(BF16)
            send(("d", k, i), sd.at[k, i - 1], rd.at[k, i - 1], dsem, (k, i - 1), ypeer(i))

    def cols_sum(k):
        value = gp[k, yrows(0), :]
        for i in (1, 3, 2):
            wait(("d", k, i))
            value = value + rd[k, i - 1].astype(F32)
        i = ORDER[k]
        if i == 0:
            own_t[...] = value
        else:
            se[i - 1] = value.astype(BF16)
            send(("e", i), se.at[i - 1], re.at[i - 1], esem, (i - 1,), hpeer(i))

    def finish(_):
        value = own_t[...]
        for i in (1, 3, 2):
            wait(("e", i))
            value = value + re[i - 1].astype(F32)
        gtok_ref[...] = value.astype(BF16)

    def weight_grads(n):
        ref, half = (hb, c) if n < 3 else (hs, sib)
        which = (1, 2, 0)[n % 3]
        if n == 3:
            for k in range(CHUNKS):
                wait(("sh_a", k))
                wait(("sh_b", k))
        cols = [jnp.concatenate(v, axis=0) for v in zip(*(
            flat(ref, k, which * NA, NA) + flat(ref, k, ga + which * nb, nb) for k in range(CHUNKS)))]
        units = jnp.concatenate(cols, axis=1)
        acted = jnp.concatenate([acts[c, plane(k), 1 if which == 0 else 0] for k in range(CHUNKS)], axis=0)
        span = pl.ds(pl.multiple_of(half * width, 128), width)
        if which == 0:
            od[span, :] = contract_first(units, acted).astype(BF16)
            kept.append(local(od.at[span, :], gd_hbm.at[span, :], osem.at[n]))
        else:
            out, hbm = ((og, gg_hbm), (ou, gu_hbm))[which - 1]
            out[:, span] = contract_first(acted, units).astype(BF16)
            kept.append(local(out.at[:, span], hbm.at[:, span], osem.at[n]))

    stages = dict(
        Z=pass_y, T=take, FA=forward_a, FB=forward_b, MA=middle_a, SA=second_a, PA=point_a, AA=across_a,
        WA=onward_a, HA=share_a, SB=second_b, MB=middle_b, PB=point_b, WB=onward_b, YB=across_b,
        HB=share_b, BA=back_a, BB=back_b, C=cols_send, D=cols_sum, E=finish, G=weight_grads)
    for item in SCHEDULE:
        stages[item[:-1]](int(item[-1]))
    for copy in sent:
        copy.wait_send()
    for copy in kept:
        copy.wait()


def local(tokens, out_grad, seq_ids, confidence, gate_weight, up_weight, down_weight):
    rows, depth = tokens.shape
    width = gate_weight.shape[1] // 2
    groups = width // 128
    nb = groups - NA
    ga, gb = 3 * NA, 3 * nb
    ha, hb = (ga + 1) // 2, (gb + 1) // 2
    total = ga + gb
    chunk = rows * NY
    k = CHUNKS
    vm, sm, dma = pltpu.VMEM, pltpu.SMEM, pltpu.SemaphoreType.DMA
    anyspace = pl.BlockSpec(memory_space=pl.ANY)
    vmspace = pl.BlockSpec(memory_space=pltpu.VMEM)
    one, two = dma((2, k)), dma((2, k, 2))
    return pl.pallas_call(
        main_kernel,
        name="exchange",
        out_shape=(
            jax.ShapeDtypeStruct((rows, depth), BF16),
            jax.ShapeDtypeStruct((depth, 2 * width), BF16),
            jax.ShapeDtypeStruct((depth, 2 * width), BF16),
            jax.ShapeDtypeStruct((2 * width, depth), BF16),
        ),
        in_specs=[anyspace] * 7,
        out_specs=(vmspace, anyspace, anyspace, anyspace),
        scratch_shapes=[
            sm(seq_ids.shape, jnp.int32),
            sm(confidence.shape, jnp.int32),
            vm((rows, depth), BF16),
            vm((2, NH, 2, chunk, depth), BF16),
            vm((2, depth, width), BF16),
            vm((2, depth, width), BF16),
            vm((2, width, depth), BF16),
            vm((k, NX, NZ, total, 16, 128), BF16),
            vm((k, NX, NZ, total, 16, 128), F32),
            vm((k, 2, NZ, ha, 16, 128), BF16),
            vm((k, 2, NZ, ha, 16, 128), BF16),
            vm((k, 2, NZ, ha, 16, 128), BF16),
            vm((k, 2, NZ, ha, 16, 128), BF16),
            vm((k, ga, 16, 128), BF16),
            vm((k, ga, 16, 128), BF16),
            vm((k, ga, 16, 128), F32),
            vm((k, NX, gb, 16, 128), BF16),
            vm((k, NX, gb, 16, 128), F32),
            vm((k, NX, gb, 16, 128), BF16),
            vm((k, 2, hb, 16, 128), BF16),
            vm((k, 2, hb, 16, 128), BF16),
            vm((k, 2, hb, 16, 128), BF16),
            vm((k, 2, hb, 16, 128), BF16),
            vm((gb, 16, 128), F32),
            vm((k, NX, NZ, total, 16, 128), BF16),
            vm((k, NX, NZ, total, 16, 128), BF16),
            vm((k, chunk, depth), F32),
            vm((k, chunk, depth), F32),
            vm((k, chunk, depth), F32),
            vm((k, 3, rows, depth), BF16),
            vm((k, 3, rows, depth), BF16),
            vm((3, rows, depth), BF16),
            vm((3, rows, depth), BF16),
            vm((rows, depth), F32),
            vm((depth, 2 * width), BF16),
            vm((depth, 2 * width), BF16),
            vm((2 * width, depth), BF16),
            dma((7,)), dma((6,)), dma((2, 3)), dma((2, 3)), dma((2, k, 3)), one,
            two, two, two, one, one, two, two, one,
            two, two, two, one, one, two, two, one,
            one, dma((2, k, 3)), dma((2, 3)),
        ],
        compiler_params=pltpu.CompilerParams(
            collective_id=0, has_side_effects=True, vmem_limit_bytes=56 << 20),
    )(seq_ids, confidence, tokens, out_grad, gate_weight, up_weight, down_weight)


def solution(mesh):
    placed = (
        P("col", "row"),
        P("col", "row"),
        P("col"),
        P(),
        P("row", "col"),
        P("row", "col"),
        P("col", "row"),
    )
    return jax.shard_map(
        local,
        mesh=mesh,
        in_specs=placed,
        out_specs=(P("col", "row"), P("row", "col"), P("row", "col"), P("col", "row")),
        check_vma=False,
    )
```

```python
import jax
import jax.numpy as jnp
from jax import lax
from jax.experimental import pallas as pl
from jax.experimental.pallas import tpu as pltpu
from jax.sharding import PartitionSpec as P

MESH = pl.DeviceIdType.MESH
BF16, F32 = jnp.bfloat16, jnp.float32
NX, NZ, NH, NY = 4, 2, 4, 4
CHUNKS = 4
ORDER = (0, 1, 3, 2)
NA = 4
DIRECT = 0
SCHEDULE = (
    "T0", "U0", "Z1", "FA0", "FB0", "Z2", "FH0", "T1", "Z3", "MA0", "SB0", "FB1", "FA1", "FH1", "T2", "MB0",
    "FA2", "FB2", "FH2", "T3", "MA1", "SB1", "FB3", "FA3", "FH3", "MA2", "SA1", "MB1", "SA0", "SB2", "MA3",
    "SB3", "SA2", "PB1", "MB2", "PA1", "PB0", "SA3", "MB3", "PA0", "WB1", "PB2", "AA1", "PA2", "PA3", "PB3",
    "YB1", "WB2", "AA2", "WB3", "AA3", "YB2", "WA1", "YB3", "WA2", "WA3", "HB1", "HB2", "YB0", "HA1", "AA0",
    "BA1", "HA2", "BB1", "HA3", "BA3", "HB3", "BB3", "C1", "BA2", "BB2", "C3", "C2", "HB0", "HA0", "BA0",
    "BB0", "D3", "G4", "C0", "D1", "D2", "G0", "G3", "G5", "G1", "G2", "D0", "E0",
)

def contract_last(left, right):
    return lax.dot_general(left, right, (((1,), (1,)), ((), ())), preferred_element_type=F32)


def contract_first(left, right):
    return lax.dot_general(left, right, (((0,), (0,)), ((), ())), preferred_element_type=F32)


def pointwise(gate, up, gh):
    sig = 1.0 / (1.0 + jnp.exp(-gate))
    silu = gate * sig
    hidden = (silu * up).astype(BF16)
    grad_pre_gate = (gh * up * sig * (1.0 + gate * (1.0 - sig))).astype(BF16)
    grad_pre_up = (gh * silu).astype(BF16)
    return hidden, grad_pre_gate, grad_pre_up


def main_kernel(
    seq_hbm, conf_hbm, tok_hbm, grad_hbm, gate_hbm, up_hbm, down_hbm,
    gtok_ref, og, ou, od,
    seq, conf, raw, acts, wg, wu, wd, part, full,
    far_a, fin_a, sum_a, mid_a, out_a, in_a, own_a,
    in_b, full_b, part_b, far_b, fin_b, sum_b, mid_b,
    tot, hb, hs, gp, gq, gr, sd, rd, se, re, own_t,
    lsem, wsem, hsem, ysem, csem, ywsem, cwsem,
    far_as, fin_as, sum_as, z_as, gz_as, gx_as, gw_as, sh_as,
    far_bs, fin_bs, sum_bs, z_bs, gz_bs, gx_bs, gw_bs, sh_bs,
    psem, dsem, esem,
):
    row, col = lax.axis_index("row"), lax.axis_index("col")
    z, x, c = row // 8, (row // 2) % 4, row % 2
    zh, y = col // 4, col % 4
    sib = 1 - c
    width = wg.shape[2]
    groups = width // 128
    nb = groups - NA
    ga, gb = 3 * NA, 3 * nb
    rows = raw.shape[0]
    right, left = (x + 1) % NX, (x + 3) % NX
    across = (x + 2) % NX

    def dev(x=x, z=z, c=c, zh=zh, y=y):
        return (z * 8 + x * 2 + c, zh * 4 + y)

    def ypeer(i):
        return dev(y=(y + i) % NY)

    def hpeer(i):
        return dev(zh=(zh + i) % NH)

    zpeer, speer = dev(z=1 - z), dev(c=sib)
    xpeers = (dev(x=right), dev(x=left))
    apeer = dev(x=across)

    sent, state, seen = [], {}, set()

    def send(key, src, dst, sems, index, peer):
        copy = pltpu.make_async_remote_copy(
            src_ref=src, dst_ref=dst, send_sem=sems.at[(0,) + index], recv_sem=sems.at[(1,) + index],
            device_id=peer, device_id_type=MESH)
        copy.start()
        sent.append(copy)
        state[key] = copy

    def wait(key):
        if key not in seen:
            seen.add(key)
            state[key].wait_recv()

    def local(src, dst, sem):
        copy = pltpu.make_async_copy(src, dst, sem)
        copy.start()
        return copy

    bar = pltpu.get_barrier_semaphore()
    peers = list(xpeers) + [apeer] + [ypeer(i) for i in (1, 2, 3)] + [hpeer(i) for i in (1, 2, 3)] + [zpeer, speer]
    for peer in peers:
        pl.semaphore_signal(bar, inc=1, device_id=peer, device_id_type=MESH)

    def yrows(i):
        return pl.ds(pl.multiple_of(((y + i) % NY) * rows, rows), rows)

    first = [
        local(seq_hbm, seq, lsem.at[0]),
        local(conf_hbm, conf, lsem.at[1]),
        local(grad_hbm, raw, lsem.at[2]),
        local(tok_hbm, acts.at[c, zh, 0, yrows(0), :], lsem.at[3]),
    ]
    mine = pl.ds(pl.multiple_of(c * width, 128), width)
    theirs = pl.ds(pl.multiple_of(sib * width, 128), width)
    loads = [
        local(gate_hbm.at[:, mine], wg.at[c], lsem.at[4]),
        local(up_hbm.at[:, mine], wu.at[c], lsem.at[5]),
        local(down_hbm.at[mine, :], wd.at[c], lsem.at[6]),
    ]
    pl.semaphore_wait(bar, len(peers))

    for i in (1, 3, 2):
        send(("y", 0, i), tok_hbm, acts.at[c, zh, 0, yrows(0), :], ysem, (0, i - 1), ypeer(i))
    send(("w", 0), gate_hbm.at[:, theirs], wg.at[c], wsem, (0,), speer)
    send(("w", 1), up_hbm.at[:, theirs], wu.at[c], wsem, (1,), speer)
    send(("w", 2), down_hbm.at[theirs, :], wd.at[c], wsem, (2,), speer)
    for copy in first:
        copy.wait()
    at = lax.broadcasted_iota(jnp.int32, (rows, 1), 0)
    factor = jnp.zeros((rows, 1), F32)
    for i in range(rows):
        factor = jnp.where(at == i, conf[seq[i]].astype(F32) * 0.25, factor)
    acts[c, zh, 1, yrows(0), :] = (raw[...].astype(F32) * factor).astype(BF16)
    block = acts.at[c, zh, 1, yrows(0), :]
    for i in (1, 3, 2):
        send(("yw", i), block, block, ywsem, (i - 1,), ypeer(i))
    block = acts.at[c, zh, :, yrows(0), :]
    for i in (1, 3, 2):
        send(("h", i), block, block, hsem, (i - 1,), hpeer(i))

    def plane(k):
        return (zh + ORDER[k]) % NH

    def pass_y(k):
        wait(("h", (NH - ORDER[k]) % NH))
        block = acts.at[c, plane(k), :, yrows(0), :]
        for i in (1, 3, 2):
            send(("y", k, i), block, block, ysem, (k, i - 1), ypeer(i))

    def take(k):
        for i in (1, 3, 2):
            wait(("y", k, i))
        got = acts.at[c, plane(k)] if k else acts.at[c, zh, 0]
        send(("c", k), got, got, csem, (k,), speer)

    def take_weighted(_):
        for i in (1, 3, 2):
            wait(("yw", i))
        got = acts.at[c, zh, 1]
        send(("cw",), got, got, cwsem, (), speer)

    def product(k, which, lo, n):
        span = pl.ds(lo * 128, n * 128)
        arr = 1 if which == 2 else 0
        t0, t1 = acts[0, plane(k), arr], acts[1, plane(k), arr]
        if which == 2:
            value = contract_last(t0, wd[0, span, :]) + contract_last(t1, wd[1, span, :])
        else:
            w = (wg, wu)[which]
            value = jnp.dot(t0, w[0, :, span], preferred_element_type=F32) + jnp.dot(
                t1, w[1, :, span], preferred_element_type=F32)
        base = which * NA if lo == 0 else ga + which * nb
        for g in range(n):
            v = value[:, g * 128 : (g + 1) * 128].reshape(NX, NZ, 16, 128)
            full[k, :, :, base + g] = v
            part[k, :, :, base + g] = v.astype(BF16)

    def halves(n, k):
        cut = (n + 1 - k % 2) // 2
        return (0, cut), (cut, n - cut)

    def send_a(k, h):
        lo, n = halves(ga, k)[h]
        send(("far_a", k, h), part.at[k, across, :, pl.ds(lo, n)], far_a.at[k, h, :, pl.ds(0, n)],
             far_as, (k, h), xpeers[h])
        d = 1 - h
        send(("fin_a", k, d), part.at[k, (right, left)[d], :, pl.ds(lo, n)],
             fin_a.at[k, d, :, pl.ds(0, n)], fin_as, (k, d), xpeers[d])

    def ready(k, which):
        wait(("c", k))
        if which == 2:
            wait(("cw",))
        wait(("w", which))
        if which not in seen:
            seen.add(which)
            loads[which].wait()

    def forward_a(k):
        for which in range(2):
            ready(k, which)
            product(k, which, 0, NA)
        send_a(k, 0)

    def forward_h(k):
        ready(k, 2)
        product(k, 2, 0, NA)
        send_a(k, 1)

    def middle_a(k):
        for d in range(2):
            lo, n = halves(ga, k)[d]
            wait(("far_a", k, d))
            value = full[k, (right, left)[d], :, lo : lo + n] + far_a[k, d, :, :n].astype(F32)
            mid_a[k, d, :, :n] = value.astype(BF16)
            span = pl.ds(0, n)
            send(("sum_a", k, d), mid_a.at[k, d, :, span], sum_a.at[k, d, :, span],
                 sum_as, (k, d), xpeers[d])

    def second_a(k):
        for d in range(2):
            wait(("fin_a", k, d))
        for d in range(2):
            wait(("sum_a", k, d))
        for zz in (1 - z, z):
            for d in range(2):
                lo, n = halves(ga, k)[d]
                value = (full[k, x, zz, lo : lo + n] + sum_a[k, d, zz, :n].astype(F32)
                         + fin_a[k, 1 - d, zz, :n].astype(F32))
                if zz is z:
                    own_a[k, lo : lo + n] = value
                else:
                    out_a[k, lo : lo + n] = value.astype(BF16)
            if zz is not z:
                send(("z_a", k), out_a.at[k], in_a.at[k], z_as, (k,), zpeer)

    def point_a(k):
        wait(("z_a", k))
        value = own_a[k] + in_a[k].astype(F32)
        results = pointwise(value[:NA], value[NA : 2 * NA], value[2 * NA :])
        for which in range(3):
            hb[k, x, z, which * NA : (which + 1) * NA] = results[which]
        block = hb.at[k, x, z, pl.ds(0, ga)]
        send(("gz_a", k), block, block, gz_as, (k,), zpeer)

    def across_a(k):
        wait(("gz_a", k))
        block = hb.at[k, x, :, pl.ds(0, ga)]
        for d in range(2):
            send(("gx_a", k, d), block, block, gx_as, (k, d), xpeers[d])
        if k == DIRECT:
            send(("gw_a", k, 0), block, block, gw_as, (k, 0), apeer)

    def onward_a(k):
        for d in range(2):
            lo, n = halves(ga, k)[d]
            wait(("gx_a", k, d))
            block = hb.at[k, (left, right)[d], :, pl.ds(lo, n)]
            send(("gw_a", k, d), block, block, gw_as, (k, d), xpeers[d])

    def arrived(far, near, k):
        for key in ((near, k, 0), (near, k, 1), (far, k, 0), (far, k, 1)):
            if key in state:
                wait(key)

    def share_a(k):
        arrived("gw_a", "gx_a", k)
        send(("sh_a", k), hb.at[k, :, :, pl.ds(0, ga)], hs.at[k, :, :, pl.ds(0, ga)], sh_as, (k,), speer)

    def forward_b(k):
        for which in range(3):
            ready(k, which)
            product(k, which, NA, nb)
        send(("z_b", k), part.at[k, :, 1 - z, pl.ds(ga, gb)], in_b.at[k], z_bs, (k,), zpeer)

    def second_b(k):
        wait(("z_b", k))
        value = full[k, :, z, ga:] + in_b[k].astype(F32)
        full_b[k] = value
        part_b[k] = value.astype(BF16)
        for d in range(2):
            lo, n = halves(gb, k)[d]
            send(("far_b", k, d), part_b.at[k, across, pl.ds(lo, n)], far_b.at[k, d, pl.ds(0, n)],
                 far_bs, (k, d), xpeers[d])
        for d in range(2):
            lo, n = halves(gb, k)[1 - d]
            send(("fin_b", k, d), part_b.at[k, (right, left)[d], pl.ds(lo, n)],
                 fin_b.at[k, d, pl.ds(0, n)], fin_bs, (k, d), xpeers[d])

    def middle_b(k):
        for d in range(2):
            lo, n = halves(gb, k)[d]
            wait(("far_b", k, d))
            value = full_b[k, (right, left)[d], lo : lo + n] + far_b[k, d, :n].astype(F32)
            mid_b[k, d, :n] = value.astype(BF16)
            span = pl.ds(0, n)
            send(("sum_b", k, d), mid_b.at[k, d, span], sum_b.at[k, d, span], sum_bs, (k, d), xpeers[d])

    def point_b(k):
        for d in range(2):
            wait(("fin_b", k, d))
        for d in range(2):
            wait(("sum_b", k, d))
        for d in range(2):
            lo, n = halves(gb, k)[d]
            tot[lo : lo + n] = (full_b[k, x, lo : lo + n] + sum_b[k, d, :n].astype(F32)
                                + fin_b[k, 1 - d, :n].astype(F32))
        results = pointwise(tot[:nb], tot[nb : 2 * nb], tot[2 * nb :])
        for which in range(3):
            hb[k, x, z, ga + which * nb : ga + (which + 1) * nb] = results[which]
        block = hb.at[k, x, z, pl.ds(ga, gb)]
        for d in range(2):
            send(("gx_b", k, d), block, block, gx_bs, (k, d), xpeers[d])
        if k == DIRECT:
            send(("gw_b", k, 0), block, block, gw_bs, (k, 0), apeer)

    def onward_b(k):
        for d in range(2):
            lo, n = halves(gb, k)[d]
            wait(("gx_b", k, d))
            block = hb.at[k, (left, right)[d], z, pl.ds(ga + lo, n)]
            send(("gw_b", k, d), block, block, gw_bs, (k, d), xpeers[d])

    def across_b(k):
        arrived("gw_b", "gx_b", k)
        block = hb.at[k, :, z, pl.ds(ga, gb)]
        send(("gz_b", k), block, block, gz_bs, (k,), zpeer)

    def share_b(k):
        wait(("gz_b", k))
        send(("sh_b", k), hb.at[k, :, :, pl.ds(ga, gb)], hs.at[k, :, :, pl.ds(ga, gb)], sh_bs, (k,), speer)

    def flat(ref, k, first, n):
        return [ref[k, :, :, first + g].reshape(NX * NZ * 16, 128) for g in range(n)]

    def back(k, base, lo, n):
        dg = jnp.concatenate(flat(hb, k, base + n, n), axis=1)
        du = jnp.concatenate(flat(hb, k, base + 2 * n, n), axis=1)
        span = pl.ds(lo * 128, n * 128)
        return [contract_last(dg, wg[h, :, span]) + contract_last(du, wu[h, :, span]) for h in (sib, c)]

    def back_a(k):
        gq[k], gp[k] = back(k, 0, 0, NA)

    def back_b(k):
        other, own = back(k, ga, NA, nb)
        gq[k] = gq[k] + other
        send(("p", k), gq.at[k], gr.at[k], psem, (k,), speer)
        gp[k] = gp[k] + own

    def cols_send(k):
        wait(("p", k))
        gp[k] = gp[k] + gr[k]
        for i in (2, 1, 3):
            sd[k, i - 1] = gp[k, yrows(i), :].astype(BF16)
            send(("d", k, i), sd.at[k, i - 1], rd.at[k, i - 1], dsem, (k, i - 1), ypeer(i))

    def cols_sum(k):
        value = gp[k, yrows(0), :]
        for i in (1, 3, 2):
            wait(("d", k, i))
            value = value + rd[k, i - 1].astype(F32)
        i = ORDER[k]
        if i == 0:
            own_t[...] = value
        else:
            se[i - 1] = value.astype(BF16)
            send(("e", i), se.at[i - 1], re.at[i - 1], esem, (i - 1,), hpeer(i))

    def finish(_):
        value = own_t[...]
        for i in (1, 3, 2):
            wait(("e", i))
            value = value + re[i - 1].astype(F32)
        gtok_ref[...] = value.astype(BF16)

    def weight_grads(n):
        ref, half = (hb, c) if n < 3 else (hs, sib)
        which = (1, 2, 0)[n % 3]
        if n >= 3:
            for k in range(CHUNKS):
                wait(("sh_a", k))
                wait(("sh_b", k))
        cols = [jnp.concatenate(v, axis=0) for v in zip(*(
            flat(ref, k, which * NA, NA) + flat(ref, k, ga + which * nb, nb) for k in range(CHUNKS)))]
        units = jnp.concatenate(cols, axis=1)
        acted = jnp.concatenate([acts[c, plane(k), 1 if which == 0 else 0] for k in range(CHUNKS)], axis=0)
        span = pl.ds(pl.multiple_of(half * width, 128), width)
        if which == 0:
            od[span, :] = contract_first(units, acted).astype(BF16)
        else:
            (og, ou)[which - 1][:, span] = contract_first(acted, units).astype(BF16)

    stages = dict(
        Z=pass_y, T=take, U=take_weighted, FA=forward_a, FH=forward_h, FB=forward_b, MA=middle_a, SA=second_a, PA=point_a, AA=across_a,
        WA=onward_a, HA=share_a, SB=second_b, MB=middle_b, PB=point_b, WB=onward_b, YB=across_b,
        HB=share_b, BA=back_a, BB=back_b, C=cols_send, D=cols_sum, E=finish, G=weight_grads)
    for item in SCHEDULE:
        stages[item[:-1]](int(item[-1]))
    for copy in sent:
        copy.wait_send()


def write_kernel(*refs):
    n = len(refs) // 2
    sem = refs[-1]
    copies = [pltpu.make_async_copy(refs[i], refs[n + i], sem.at[i]) for i in range(n)]
    for copy in copies:
        copy.start()
    for copy in copies:
        copy.wait()


def local(tokens, out_grad, seq_ids, confidence, gate_weight, up_weight, down_weight):
    rows, depth = tokens.shape
    width = gate_weight.shape[1] // 2
    groups = width // 128
    nb = groups - NA
    ga, gb = 3 * NA, 3 * nb
    ha, hb = (ga + 1) // 2, (gb + 1) // 2
    total = ga + gb
    chunk = rows * NY
    k = CHUNKS
    vm, sm, dma = pltpu.VMEM, pltpu.SMEM, pltpu.SemaphoreType.DMA
    anyspace = pl.BlockSpec(memory_space=pl.ANY)
    vmspace = pl.BlockSpec(memory_space=pltpu.VMEM)
    one, two = dma((2, k)), dma((2, k, 2))
    shapes = (rows, depth), (depth, 2 * width), (depth, 2 * width), (2 * width, depth)
    results = pl.pallas_call(
        main_kernel,
        name="exchange",
        out_shape=tuple(vm(shape, BF16) for shape in shapes),
        in_specs=[anyspace] * 7,
        out_specs=(vmspace,) * 4,
        scratch_shapes=[
            sm(seq_ids.shape, jnp.int32),
            sm(confidence.shape, jnp.int32),
            vm((rows, depth), BF16),
            vm((2, NH, 2, chunk, depth), BF16),
            vm((2, depth, width), BF16),
            vm((2, depth, width), BF16),
            vm((2, width, depth), BF16),
            vm((k, NX, NZ, total, 16, 128), BF16),
            vm((k, NX, NZ, total, 16, 128), F32),
            vm((k, 2, NZ, ha, 16, 128), BF16),
            vm((k, 2, NZ, ha, 16, 128), BF16),
            vm((k, 2, NZ, ha, 16, 128), BF16),
            vm((k, 2, NZ, ha, 16, 128), BF16),
            vm((k, ga, 16, 128), BF16),
            vm((k, ga, 16, 128), BF16),
            vm((k, ga, 16, 128), F32),
            vm((k, NX, gb, 16, 128), BF16),
            vm((k, NX, gb, 16, 128), F32),
            vm((k, NX, gb, 16, 128), BF16),
            vm((k, 2, hb, 16, 128), BF16),
            vm((k, 2, hb, 16, 128), BF16),
            vm((k, 2, hb, 16, 128), BF16),
            vm((k, 2, hb, 16, 128), BF16),
            vm((gb, 16, 128), F32),
            vm((k, NX, NZ, total, 16, 128), BF16),
            vm((k, NX, NZ, total, 16, 128), BF16),
            vm((k, chunk, depth), F32),
            vm((k, chunk, depth), F32),
            vm((k, chunk, depth), F32),
            vm((k, 3, rows, depth), BF16),
            vm((k, 3, rows, depth), BF16),
            vm((3, rows, depth), BF16),
            vm((3, rows, depth), BF16),
            vm((rows, depth), F32),
            dma((7,)), dma((2, 3)), dma((2, 3)), dma((2, k, 3)), one, dma((2, 3)), dma((2,)),
            two, two, two, one, one, two, two, one,
            two, two, two, one, one, two, two, one,
            one, dma((2, k, 3)), dma((2, 3)),
        ],
        compiler_params=pltpu.CompilerParams(
            collective_id=0, has_side_effects=True, vmem_limit_bytes=48 << 20),
    )(*(pltpu.with_memory_space_constraint(v, pltpu.HBM) for v in (
        seq_ids, confidence, tokens, out_grad, gate_weight, up_weight, down_weight)))
    return pl.pallas_call(
        write_kernel,
        name="write_out",
        out_shape=tuple(jax.ShapeDtypeStruct(shape, BF16) for shape in shapes),
        in_specs=[vmspace] * 4,
        out_specs=(anyspace,) * 4,
        scratch_shapes=[dma((4,))],
        compiler_params=pltpu.CompilerParams(vmem_limit_bytes=16 << 20),
    )(*(pltpu.with_memory_space_constraint(v, pltpu.VMEM) for v in results))


def solution(mesh):
    placed = (
        P("col", "row"),
        P("col", "row"),
        P("col"),
        P(),
        P("row", "col"),
        P("row", "col"),
        P("col", "row"),
    )
    return jax.shard_map(
        local,
        mesh=mesh,
        in_specs=placed,
        out_specs=(P("col", "row"), P("row", "col"), P("row", "col"), P("col", "row")),
        check_vma=False,
    )
```

```python
import jax
import jax.numpy as jnp
from jax import lax
from jax.experimental import pallas as pl
from jax.experimental.pallas import tpu as pltpu
from jax.sharding import PartitionSpec as P

MESH = pl.DeviceIdType.MESH
BF16, F32 = jnp.bfloat16, jnp.float32
NX, NZ, NH, NY = 4, 2, 4, 4
CHUNKS = 4
ORDER = (0, 1, 3, 2)
NA = 4
DIRECT = 0
SCHEDULE = (
    "Z2", "T0", "Z1", "U0", "FA0", "V2", "Z3", "FH0", "FB0", "T2", "V3", "T1", "FA2", "V1", "U2", "MA0",
    "FA1", "FB2", "T3", "FH2", "U3", "SB0", "FA3", "FB3", "U1", "FH3", "MA2", "FH1", "FB1", "SB2", "MA3",
    "MA1", "SA2", "SA0", "MB2", "SB3", "MB0", "SA3", "SB1", "SA1", "PB2", "PA2", "MB3", "MB1", "PA3", "PA1",
    "WB2", "PB3", "AA2", "PB1", "AA3", "YB2", "WB3", "AA1", "WA2", "WB1", "WA3", "HB2", "YB3", "PB0", "WA1",
    "PA0", "HA2", "BA2", "YB1", "BB2", "HB3", "HA3", "BA3", "BB3", "WB0", "C2", "AA0", "YB0", "HB1", "HA1",
    "BA1", "BB1", "C3", "C1", "HB0", "BB0", "HA0", "BA0", "D3", "D2", "C0", "D1", "G2", "G1", "G0", "G3",
    "G5", "G4", "D0", "E0",
)

def contract_last(left, right):
    return lax.dot_general(left, right, (((1,), (1,)), ((), ())), preferred_element_type=F32)


def contract_first(left, right):
    return lax.dot_general(left, right, (((0,), (0,)), ((), ())), preferred_element_type=F32)


def pointwise(gate, up, gh):
    sig = 1.0 / (1.0 + jnp.exp(-gate))
    silu = gate * sig
    hidden = (silu * up).astype(BF16)
    grad_pre_gate = (gh * up * sig * (1.0 + gate * (1.0 - sig))).astype(BF16)
    grad_pre_up = (gh * silu).astype(BF16)
    return hidden, grad_pre_gate, grad_pre_up


def main_kernel(
    seq_hbm, conf_hbm, tok_hbm, grad_hbm, gate_hbm, up_hbm, down_hbm,
    gtok_ref, og, ou, od,
    seq, conf, raw, acts, wg, wu, wd, part, full,
    far_a, fin_a, sum_a, mid_a, out_a, in_a, own_a,
    in_b, full_b, part_b, far_b, fin_b, sum_b, mid_b,
    tot, hb, hs, gp, gq, gr, sd, rd, se, re, own_t,
    lsem, wsem, hsem, ysem, csem,
    far_as, fin_as, sum_as, z_as, gz_as, gx_as, gw_as, sh_as,
    far_bs, fin_bs, sum_bs, z_bs, gz_bs, gx_bs, gw_bs, sh_bs,
    psem, dsem, esem,
):
    row, col = lax.axis_index("row"), lax.axis_index("col")
    z, x, c = row // 8, (row // 2) % 4, row % 2
    zh, y = col // 4, col % 4
    sib = 1 - c
    width = wg.shape[2]
    groups = width // 128
    nb = groups - NA
    ga, gb = 3 * NA, 3 * nb
    rows = raw.shape[0]
    right, left = (x + 1) % NX, (x + 3) % NX
    across = (x + 2) % NX

    def dev(x=x, z=z, c=c, zh=zh, y=y):
        return (z * 8 + x * 2 + c, zh * 4 + y)

    def ypeer(i):
        return dev(y=(y + i) % NY)

    def hpeer(i):
        return dev(zh=(zh + i) % NH)

    zpeer, speer = dev(z=1 - z), dev(c=sib)
    xpeers = (dev(x=right), dev(x=left))
    apeer = dev(x=across)

    sent, state, seen, begun = [], {}, set(), set()

    def send(key, src, dst, sems, index, peer):
        copy = pltpu.make_async_remote_copy(
            src_ref=src, dst_ref=dst, send_sem=sems.at[(0,) + index], recv_sem=sems.at[(1,) + index],
            device_id=peer, device_id_type=MESH)
        copy.start()
        sent.append(copy)
        state[key] = copy

    def wait(key):
        if key not in seen:
            seen.add(key)
            state[key].wait_recv()

    def local(src, dst, sem):
        copy = pltpu.make_async_copy(src, dst, sem)
        copy.start()
        return copy

    bar = pltpu.get_barrier_semaphore()
    peers = list(xpeers) + [apeer] + [ypeer(i) for i in (1, 2, 3)] + [hpeer(i) for i in (1, 2, 3)] + [zpeer, speer]
    for peer in peers:
        pl.semaphore_signal(bar, inc=1, device_id=peer, device_id_type=MESH)

    def yrows(i):
        return pl.ds(pl.multiple_of(((y + i) % NY) * rows, rows), rows)

    first = [
        local(seq_hbm, seq, lsem.at[0]),
        local(conf_hbm, conf, lsem.at[1]),
        local(grad_hbm, raw, lsem.at[2]),
        local(tok_hbm, acts.at[c, zh, 0, yrows(0), :], lsem.at[3]),
    ]
    mine = pl.ds(pl.multiple_of(c * width, 128), width)
    theirs = pl.ds(pl.multiple_of(sib * width, 128), width)
    loads = [
        local(gate_hbm.at[:, mine], wg.at[c], lsem.at[4]),
        local(up_hbm.at[:, mine], wu.at[c], lsem.at[5]),
        local(down_hbm.at[mine, :], wd.at[c], lsem.at[6]),
    ]
    pl.semaphore_wait(bar, len(peers))

    def plane(k):
        return (zh + ORDER[k]) % NH

    def block_of(k, arr):
        return acts.at[c, plane(k), arr, yrows(0), :]

    def to_y(k, arr, src):
        for i in (1, 3, 2):
            send(("y", arr, k, i), src, block_of(k, arr), ysem, (arr, k, i - 1), ypeer(i))

    def to_h(arr, src):
        for i in (1, 3, 2):
            send(("h", arr, i), src, block_of(0, arr), hsem, (arr, i - 1), hpeer(i))

    to_y(0, 0, tok_hbm)
    to_h(0, tok_hbm)
    send(("w", 0), gate_hbm.at[:, theirs], wg.at[c], wsem, (0,), speer)
    send(("w", 1), up_hbm.at[:, theirs], wu.at[c], wsem, (1,), speer)
    send(("w", 2), down_hbm.at[theirs, :], wd.at[c], wsem, (2,), speer)
    for copy in first:
        copy.wait()
    at = lax.broadcasted_iota(jnp.int32, (rows, 1), 0)
    factor = jnp.zeros((rows, 1), F32)
    for i in range(rows):
        factor = jnp.where(at == i, conf[seq[i]].astype(F32) * 0.25, factor)
    acts[c, zh, 1, yrows(0), :] = (raw[...].astype(F32) * factor).astype(BF16)
    to_y(0, 1, block_of(0, 1))
    to_h(1, block_of(0, 1))

    def pass_y(k, arr=0):
        wait(("h", arr, (NH - ORDER[k]) % NH))
        to_y(k, arr, block_of(k, arr))

    def pass_weighted(k):
        pass_y(k, 1)

    def take(k, arr=0):
        for i in (1, 3, 2):
            wait(("y", arr, k, i))
        got = acts.at[c, plane(k), arr]
        send(("c", arr, k), got, got, csem, (arr, k), speer)

    def take_weighted(k):
        take(k, 1)

    def product(k, which, lo, n):
        span = pl.ds(lo * 128, n * 128)
        arr = 1 if which == 2 else 0
        t0, t1 = acts[0, plane(k), arr], acts[1, plane(k), arr]
        if which == 2:
            value = contract_last(t0, wd[0, span, :]) + contract_last(t1, wd[1, span, :])
        else:
            w = (wg, wu)[which]
            value = jnp.dot(t0, w[0, :, span], preferred_element_type=F32) + jnp.dot(
                t1, w[1, :, span], preferred_element_type=F32)
        base = which * NA if lo == 0 else ga + which * nb
        for g in range(n):
            v = value[:, g * 128 : (g + 1) * 128].reshape(NX, NZ, 16, 128)
            full[k, :, :, base + g] = v
            part[k, :, :, base + g] = v.astype(BF16)

    def halves(n, k):
        cut = (n + 1 - k % 2) // 2
        return (0, cut), (cut, n - cut)

    def send_a(k, h):
        lo, n = halves(ga, k)[h]
        send(("far_a", k, h), part.at[k, across, :, pl.ds(lo, n)], far_a.at[k, h, :, pl.ds(0, n)],
             far_as, (k, h), xpeers[h])
        d = 1 - h
        send(("fin_a", k, d), part.at[k, (right, left)[d], :, pl.ds(lo, n)],
             fin_a.at[k, d, :, pl.ds(0, n)], fin_as, (k, d), xpeers[d])

    def ready(k, which):
        wait(("c", 1 if which == 2 else 0, k))
        wait(("w", which))
        if which not in seen:
            seen.add(which)
            loads[which].wait()

    def forward_a(k):
        for which in range(2):
            ready(k, which)
            product(k, which, 0, NA)
        send_a(k, 0)

    def forward_h(k):
        ready(k, 2)
        product(k, 2, 0, NA)
        send_a(k, 1)

    def middle_a(k):
        for d in range(2):
            lo, n = halves(ga, k)[d]
            wait(("far_a", k, d))
            value = full[k, (right, left)[d], :, lo : lo + n] + far_a[k, d, :, :n].astype(F32)
            mid_a[k, d, :, :n] = value.astype(BF16)
            span = pl.ds(0, n)
            send(("sum_a", k, d), mid_a.at[k, d, :, span], sum_a.at[k, d, :, span],
                 sum_as, (k, d), xpeers[d])

    def second_a(k):
        for d in range(2):
            wait(("fin_a", k, d))
        for d in range(2):
            wait(("sum_a", k, d))
        for zz in (1 - z, z):
            for d in range(2):
                lo, n = halves(ga, k)[d]
                value = (full[k, x, zz, lo : lo + n] + sum_a[k, d, zz, :n].astype(F32)
                         + fin_a[k, 1 - d, zz, :n].astype(F32))
                if zz is z:
                    own_a[k, lo : lo + n] = value
                else:
                    out_a[k, lo : lo + n] = value.astype(BF16)
            if zz is not z:
                send(("z_a", k), out_a.at[k], in_a.at[k], z_as, (k,), zpeer)

    def point_a(k):
        wait(("z_a", k))
        value = own_a[k] + in_a[k].astype(F32)
        results = pointwise(value[:NA], value[NA : 2 * NA], value[2 * NA :])
        for which in range(3):
            hb[k, x, z, which * NA : (which + 1) * NA] = results[which]
        block = hb.at[k, x, z, pl.ds(0, ga)]
        send(("gz_a", k), block, block, gz_as, (k,), zpeer)
        along_x(k, block, 0)

    def along_x(k, block, part_of):
        for d in range(2):
            send(("gx_a", k, d, part_of), block, block, gx_as, (k, d, part_of), xpeers[d])
        if k == DIRECT:
            send(("gw_a", k, part_of), block, block, gw_as, (k, part_of), apeer)

    def across_a(k):
        wait(("gz_a", k))
        along_x(k, hb.at[k, x, 1 - z, pl.ds(0, ga)], 1)

    def onward_a(k):
        for d in range(2):
            lo, n = halves(ga, k)[d]
            for part_of in range(2):
                wait(("gx_a", k, d, part_of))
            block = hb.at[k, (left, right)[d], :, pl.ds(lo, n)]
            send(("gw_a", k, d), block, block, gw_as, (k, d), xpeers[d])

    def share_a(k):
        for d in range(2):
            for part_of in range(2):
                wait(("gx_a", k, d, part_of))
            wait(("gw_a", k, d))
        send(("sh_a", k), hb.at[k, :, :, pl.ds(0, ga)], hs.at[k, :, :, pl.ds(0, ga)], sh_as, (k,), speer)

    def forward_b(k):
        for which in range(3):
            ready(k, which)
            product(k, which, NA, nb)
        send(("z_b", k), part.at[k, :, 1 - z, pl.ds(ga, gb)], in_b.at[k], z_bs, (k,), zpeer)

    def second_b(k):
        wait(("z_b", k))
        value = full[k, :, z, ga:] + in_b[k].astype(F32)
        full_b[k] = value
        part_b[k] = value.astype(BF16)
        for d in range(2):
            lo, n = halves(gb, k)[d]
            send(("far_b", k, d), part_b.at[k, across, pl.ds(lo, n)], far_b.at[k, d, pl.ds(0, n)],
                 far_bs, (k, d), xpeers[d])
        for d in range(2):
            lo, n = halves(gb, k)[1 - d]
            send(("fin_b", k, d), part_b.at[k, (right, left)[d], pl.ds(lo, n)],
                 fin_b.at[k, d, pl.ds(0, n)], fin_bs, (k, d), xpeers[d])

    def middle_b(k):
        for d in range(2):
            lo, n = halves(gb, k)[d]
            wait(("far_b", k, d))
            value = full_b[k, (right, left)[d], lo : lo + n] + far_b[k, d, :n].astype(F32)
            mid_b[k, d, :n] = value.astype(BF16)
            span = pl.ds(0, n)
            send(("sum_b", k, d), mid_b.at[k, d, span], sum_b.at[k, d, span], sum_bs, (k, d), xpeers[d])

    def point_b(k):
        for d in range(2):
            wait(("fin_b", k, d))
        for d in range(2):
            wait(("sum_b", k, d))
        for d in range(2):
            lo, n = halves(gb, k)[d]
            tot[lo : lo + n] = (full_b[k, x, lo : lo + n] + sum_b[k, d, :n].astype(F32)
                                + fin_b[k, 1 - d, :n].astype(F32))
        results = pointwise(tot[:nb], tot[nb : 2 * nb], tot[2 * nb :])
        for which in range(3):
            hb[k, x, z, ga + which * nb : ga + (which + 1) * nb] = results[which]
        block = hb.at[k, x, z, pl.ds(ga, gb)]
        for d in range(2):
            send(("gx_b", k, d), block, block, gx_bs, (k, d), xpeers[d])
        send(("gz_b", k, 0), block, block, gz_bs, (k, 0), zpeer)
        if k == DIRECT:
            send(("gw_b", k, 0), block, block, gw_bs, (k, 0), apeer)

    def onward_b(k):
        for d in range(2):
            wait(("gx_b", k, d))
            if k != DIRECT:
                lo, n = halves(gb, k)[d]
                block = hb.at[k, (left, right)[d], z, pl.ds(ga + lo, n)]
                send(("gw_b", k, d), block, block, gw_bs, (k, d), xpeers[d])
        for d in range(2):
            block = hb.at[k, (left, right)[d], z, pl.ds(ga, gb)]
            send(("gz_b", k, 1 + d), block, block, gz_bs, (k, 1 + d), zpeer)

    def across_b(k):
        for d in range(1 if k == DIRECT else 2):
            wait(("gw_b", k, d))
        block = hb.at[k, across, z, pl.ds(ga, gb)]
        send(("gz_b", k, 3), block, block, gz_bs, (k, 3), zpeer)

    def share_b(k):
        for i in range(4):
            wait(("gz_b", k, i))
        send(("sh_b", k), hb.at[k, :, :, pl.ds(ga, gb)], hs.at[k, :, :, pl.ds(ga, gb)], sh_bs, (k,), speer)

    def flat(ref, k, first, n):
        return [ref[k, :, :, first + g].reshape(NX * NZ * 16, 128) for g in range(n)]

    def back(k, base, lo, n):
        dg = jnp.concatenate(flat(hb, k, base + n, n), axis=1)
        du = jnp.concatenate(flat(hb, k, base + 2 * n, n), axis=1)
        span = pl.ds(lo * 128, n * 128)
        again = k in begun
        begun.add(k)
        for h, ref in ((sib, gq), (c, gp)):
            value = contract_last(dg, wg[h, :, span]) + contract_last(du, wu[h, :, span])
            ref[k] = ref[k] + value if again else value
            if again and ref is gq:
                send(("p", k), gq.at[k], gr.at[k], psem, (k,), speer)

    def back_a(k):
        back(k, 0, 0, NA)

    def back_b(k):
        back(k, ga, NA, nb)

    def cols_send(k):
        wait(("p", k))
        gp[k] = gp[k] + gr[k]
        for i in (2, 1, 3):
            sd[k, i - 1] = gp[k, yrows(i), :].astype(BF16)
            send(("d", k, i), sd.at[k, i - 1], rd.at[k, i - 1], dsem, (k, i - 1), ypeer(i))

    def cols_sum(k):
        value = gp[k, yrows(0), :]
        for i in (1, 3, 2):
            wait(("d", k, i))
            value = value + rd[k, i - 1].astype(F32)
        i = ORDER[k]
        if i == 0:
            own_t[...] = value
        else:
            se[i - 1] = value.astype(BF16)
            send(("e", i), se.at[i - 1], re.at[i - 1], esem, (i - 1,), hpeer(i))

    def finish(_):
        value = own_t[...]
        for i in (1, 3, 2):
            wait(("e", i))
            value = value + re[i - 1].astype(F32)
        gtok_ref[...] = value.astype(BF16)

    def weight_grads(n):
        ref, half = (hb, c) if n < 3 else (hs, sib)
        which = (1, 2, 0)[n % 3]
        if n >= 3:
            for k in range(CHUNKS):
                wait(("sh_a", k))
                wait(("sh_b", k))
        cols = [jnp.concatenate(v, axis=0) for v in zip(*(
            flat(ref, k, which * NA, NA) + flat(ref, k, ga + which * nb, nb) for k in range(CHUNKS)))]
        units = jnp.concatenate(cols, axis=1)
        acted = jnp.concatenate([acts[c, plane(k), 1 if which == 0 else 0] for k in range(CHUNKS)], axis=0)
        span = pl.ds(pl.multiple_of(half * width, 128), width)
        if which == 0:
            od[span, :] = contract_first(units, acted).astype(BF16)
        else:
            (og, ou)[which - 1][:, span] = contract_first(acted, units).astype(BF16)

    stages = dict(
        Z=pass_y, V=pass_weighted, T=take, U=take_weighted, FA=forward_a, FH=forward_h, FB=forward_b, MA=middle_a, SA=second_a, PA=point_a, AA=across_a,
        WA=onward_a, HA=share_a, SB=second_b, MB=middle_b, PB=point_b, WB=onward_b, YB=across_b,
        HB=share_b, BA=back_a, BB=back_b, C=cols_send, D=cols_sum, E=finish, G=weight_grads)
    for item in SCHEDULE:
        for copy in sent[:4]:
            if len(sent) > 30:
                sent.remove(copy)
                copy.wait_send()
        stages[item[:-1]](int(item[-1]))
    for copy in sent:
        copy.wait_send()


def write_kernel(*refs):
    n = len(refs) // 2
    sem = refs[-1]
    copies = [pltpu.make_async_copy(refs[i], refs[n + i], sem.at[i]) for i in range(n)]
    for copy in copies:
        copy.start()
    for copy in copies:
        copy.wait()


def local(tokens, out_grad, seq_ids, confidence, gate_weight, up_weight, down_weight):
    rows, depth = tokens.shape
    width = gate_weight.shape[1] // 2
    groups = width // 128
    nb = groups - NA
    ga, gb = 3 * NA, 3 * nb
    ha, hb = (ga + 1) // 2, (gb + 1) // 2
    total = ga + gb
    chunk = rows * NY
    k = CHUNKS
    vm, sm, dma = pltpu.VMEM, pltpu.SMEM, pltpu.SemaphoreType.DMA
    anyspace = pl.BlockSpec(memory_space=pl.ANY)
    vmspace = pl.BlockSpec(memory_space=pltpu.VMEM)
    one, two = dma((2, k)), dma((2, k, 2))
    shapes = (rows, depth), (depth, 2 * width), (depth, 2 * width), (2 * width, depth)
    results = pl.pallas_call(
        main_kernel,
        name="exchange",
        out_shape=tuple(vm(shape, BF16) for shape in shapes),
        in_specs=[anyspace] * 7,
        out_specs=(vmspace,) * 4,
        scratch_shapes=[
            sm(seq_ids.shape, jnp.int32),
            sm(confidence.shape, jnp.int32),
            vm((rows, depth), BF16),
            vm((2, NH, 2, chunk, depth), BF16),
            vm((2, depth, width), BF16),
            vm((2, depth, width), BF16),
            vm((2, width, depth), BF16),
            vm((k, NX, NZ, total, 16, 128), BF16),
            vm((k, NX, NZ, total, 16, 128), F32),
            vm((k, 2, NZ, ha, 16, 128), BF16),
            vm((k, 2, NZ, ha, 16, 128), BF16),
            vm((k, 2, NZ, ha, 16, 128), BF16),
            vm((k, 2, NZ, ha, 16, 128), BF16),
            vm((k, ga, 16, 128), BF16),
            vm((k, ga, 16, 128), BF16),
            vm((k, ga, 16, 128), F32),
            vm((k, NX, gb, 16, 128), BF16),
            vm((k, NX, gb, 16, 128), F32),
            vm((k, NX, gb, 16, 128), BF16),
            vm((k, 2, hb, 16, 128), BF16),
            vm((k, 2, hb, 16, 128), BF16),
            vm((k, 2, hb, 16, 128), BF16),
            vm((k, 2, hb, 16, 128), BF16),
            vm((gb, 16, 128), F32),
            vm((k, NX, NZ, total, 16, 128), BF16),
            vm((k, NX, NZ, total, 16, 128), BF16),
            vm((k, chunk, depth), F32),
            vm((k, chunk, depth), F32),
            vm((k, chunk, depth), F32),
            vm((k, 3, rows, depth), BF16),
            vm((k, 3, rows, depth), BF16),
            vm((3, rows, depth), BF16),
            vm((3, rows, depth), BF16),
            vm((rows, depth), F32),
            dma((7,)), dma((2, 3)), dma((2, 2, 3)), dma((2, 2, k, 3)), dma((2, 2, k)),
            two, two, two, one, one, dma((2, k, 2, 2)), two, one,
            two, two, two, one, dma((2, k, 4)), two, two, one,
            one, dma((2, k, 3)), dma((2, 3)),
        ],
        compiler_params=pltpu.CompilerParams(
            collective_id=0, has_side_effects=True, vmem_limit_bytes=48 << 20),
    )(*(pltpu.with_memory_space_constraint(v, pltpu.HBM) for v in (
        seq_ids, confidence, tokens, out_grad, gate_weight, up_weight, down_weight)))
    return pl.pallas_call(
        write_kernel,
        name="write_out",
        out_shape=tuple(jax.ShapeDtypeStruct(shape, BF16) for shape in shapes),
        in_specs=[vmspace] * 4,
        out_specs=(anyspace,) * 4,
        scratch_shapes=[dma((4,))],
        compiler_params=pltpu.CompilerParams(vmem_limit_bytes=16 << 20),
    )(*(pltpu.with_memory_space_constraint(v, pltpu.VMEM) for v in results))


def solution(mesh):
    placed = (
        P("col", "row"),
        P("col", "row"),
        P("col"),
        P(),
        P("row", "col"),
        P("row", "col"),
        P("col", "row"),
    )
    return jax.shard_map(
        local,
        mesh=mesh,
        in_specs=placed,
        out_specs=(P("col", "row"), P("row", "col"), P("row", "col"), P("col", "row")),
        check_vma=False,
    )
```

```python
import jax
import jax.numpy as jnp
from jax import lax
from jax.experimental import pallas as pl
from jax.experimental.pallas import tpu as pltpu
from jax.sharding import PartitionSpec as P

MESH = pl.DeviceIdType.MESH
BF16, F32 = jnp.bfloat16, jnp.float32
NX, NZ, NH, NY = 4, 2, 4, 4
CHUNKS = 4
ORDER = (0, 3, 1, 2)
NA = 4
DIRECT = 0
SCHEDULE = (
    "Z1", "T0", "Z2", "U0", "FA0", "V1", "FH0", "Z3", "FB0", "T1", "V3", "V2", "T2", "MA0", "FA1", "U1",
    "FA2", "T3", "FB1", "FH1", "U3", "FA3", "FH3", "U2", "FB3", "MA1", "FH2", "SB1", "FB2", "MA3", "SB0",
    "MB1", "MA2", "SA1", "SB3", "SA3", "MB0", "PB1", "SB2", "SA2", "MB3", "PA1", "PA3", "WB1", "MB2", "PB3",
    "PA2", "AA3", "YB1", "PB2", "SA0", "WB3", "AA1", "AA2", "WA3", "HB1", "YB3", "WB2", "WA1", "PB0", "WA2",
    "PA0", "HA3", "BA3", "HB3", "BB3", "HA1", "YB2", "BA1", "WB0", "C3", "BB1", "AA0", "YB0", "HA2", "BA2",
    "HB2", "BB2", "C1", "C2", "HB0", "BB0", "D3", "HA0", "BA0", "G1", "D1", "C0", "D2", "G5", "G4", "G0",
    "G2", "G3", "D0", "E0",
)

def contract_last(left, right):
    return lax.dot_general(left, right, (((1,), (1,)), ((), ())), preferred_element_type=F32)


def contract_first(left, right):
    return lax.dot_general(left, right, (((0,), (0,)), ((), ())), preferred_element_type=F32)


def pointwise(gate, up, gh):
    sig = 1.0 / (1.0 + jnp.exp(-gate))
    silu = gate * sig
    hidden = (silu * up).astype(BF16)
    grad_pre_gate = (gh * up * sig * (1.0 + gate * (1.0 - sig))).astype(BF16)
    grad_pre_up = (gh * silu).astype(BF16)
    return hidden, grad_pre_gate, grad_pre_up


def main_kernel(
    seq_hbm, conf_hbm, tok_hbm, grad_hbm, gate_hbm, up_hbm, down_hbm,
    gtok_ref, og, ou, od,
    seq, conf, raw, acts, wg, wu, wd, part, full,
    far_a, fin_a, sum_a, mid_a, out_a, in_a, own_a,
    in_b, full_b, part_b, far_b, fin_b, sum_b, mid_b,
    tot, hb, hs, gp, gq, gr, sd, rd, se, re, own_t,
    lsem, wsem, hsem, ysem, csem,
    far_as, fin_as, sum_as, z_as, gz_as, gx_as, gw_as, sh_as,
    far_bs, fin_bs, sum_bs, z_bs, gz_bs, gx_bs, gw_bs, sh_bs,
    psem, dsem, esem,
):
    row, col = lax.axis_index("row"), lax.axis_index("col")
    z, x, c = row // 8, (row // 2) % 4, row % 2
    zh, y = col // 4, col % 4
    sib = 1 - c
    width = wg.shape[2]
    groups = width // 128
    nb = groups - NA
    ga, gb = 3 * NA, 3 * nb
    rows = raw.shape[0]
    right, left = (x + 1) % NX, (x + 3) % NX
    across = (x + 2) % NX

    def dev(x=x, z=z, c=c, zh=zh, y=y):
        return (z * 8 + x * 2 + c, zh * 4 + y)

    def ypeer(i):
        return dev(y=(y + i) % NY)

    def hpeer(i):
        return dev(zh=(zh + i) % NH)

    zpeer, speer = dev(z=1 - z), dev(c=sib)
    xpeers = (dev(x=right), dev(x=left))
    apeer = dev(x=across)

    sent, state, seen, begun = [], {}, set(), set()

    def send(key, src, dst, sems, index, peer):
        copy = pltpu.make_async_remote_copy(
            src_ref=src, dst_ref=dst, send_sem=sems.at[(0,) + index], recv_sem=sems.at[(1,) + index],
            device_id=peer, device_id_type=MESH)
        copy.start()
        sent.append(copy)
        state[key] = copy

    def wait(key):
        if key not in seen:
            seen.add(key)
            state[key].wait_recv()

    def local(src, dst, sem):
        copy = pltpu.make_async_copy(src, dst, sem)
        copy.start()
        return copy

    bar = pltpu.get_barrier_semaphore()
    peers = list(xpeers) + [apeer] + [ypeer(i) for i in (1, 2, 3)] + [hpeer(i) for i in (1, 2, 3)] + [zpeer, speer]
    for peer in peers:
        pl.semaphore_signal(bar, inc=1, device_id=peer, device_id_type=MESH)

    def yrows(i):
        return pl.ds(pl.multiple_of(((y + i) % NY) * rows, rows), rows)

    first = [
        local(seq_hbm, seq, lsem.at[0]),
        local(conf_hbm, conf, lsem.at[1]),
        local(grad_hbm, raw, lsem.at[2]),
        local(tok_hbm, acts.at[c, zh, 0, yrows(0), :], lsem.at[3]),
    ]
    mine = pl.ds(pl.multiple_of(c * width, 128), width)
    theirs = pl.ds(pl.multiple_of(sib * width, 128), width)
    loads = [
        local(gate_hbm.at[:, mine], wg.at[c], lsem.at[4]),
        local(up_hbm.at[:, mine], wu.at[c], lsem.at[5]),
        local(down_hbm.at[mine, :], wd.at[c], lsem.at[6]),
    ]
    pl.semaphore_wait(bar, len(peers))

    def plane(k):
        return (zh + ORDER[k]) % NH

    def block_of(k, arr):
        return acts.at[c, plane(k), arr, yrows(0), :]

    def to_y(k, arr, src):
        for i in (1, 3, 2):
            send(("y", arr, k, i), src, block_of(k, arr), ysem, (arr, k, i - 1), ypeer(i))

    def to_h(arr, src):
        for i in (1, 3, 2):
            send(("h", arr, i), src, block_of(0, arr), hsem, (arr, i - 1), hpeer(i))

    to_y(0, 0, tok_hbm)
    to_h(0, tok_hbm)
    send(("w", 0), gate_hbm.at[:, theirs], wg.at[c], wsem, (0,), speer)
    send(("w", 1), up_hbm.at[:, theirs], wu.at[c], wsem, (1,), speer)
    send(("w", 2), down_hbm.at[theirs, :], wd.at[c], wsem, (2,), speer)
    for copy in first:
        copy.wait()
    at = lax.broadcasted_iota(jnp.int32, (rows, 1), 0)
    factor = jnp.zeros((rows, 1), F32)
    for i in range(rows):
        factor = jnp.where(at == i, conf[seq[i]].astype(F32) * 0.25, factor)
    acts[c, zh, 1, yrows(0), :] = (raw[...].astype(F32) * factor).astype(BF16)
    to_y(0, 1, block_of(0, 1))
    to_h(1, block_of(0, 1))

    def pass_y(k, arr=0):
        wait(("h", arr, (NH - ORDER[k]) % NH))
        to_y(k, arr, block_of(k, arr))

    def pass_weighted(k):
        pass_y(k, 1)

    def take(k, arr=0):
        for i in (1, 3, 2):
            wait(("y", arr, k, i))
        got = acts.at[c, plane(k), arr]
        send(("c", arr, k), got, got, csem, (arr, k), speer)

    def take_weighted(k):
        take(k, 1)

    def product(k, which, lo, n):
        span = pl.ds(lo * 128, n * 128)
        arr = 1 if which == 2 else 0
        t0, t1 = acts[0, plane(k), arr], acts[1, plane(k), arr]
        if which == 2:
            value = contract_last(t0, wd[0, span, :]) + contract_last(t1, wd[1, span, :])
        else:
            w = (wg, wu)[which]
            value = jnp.dot(t0, w[0, :, span], preferred_element_type=F32) + jnp.dot(
                t1, w[1, :, span], preferred_element_type=F32)
        base = which * NA if lo == 0 else ga + which * nb
        for g in range(n):
            v = value[:, g * 128 : (g + 1) * 128].reshape(NX, NZ, 16, 128)
            full[k, :, :, base + g] = v
            part[k, :, :, base + g] = v.astype(BF16)

    def halves(n, k):
        cut = (n + 1 - k % 2) // 2
        return (0, cut), (cut, n - cut)

    def send_a(k, h):
        lo, n = halves(ga, k)[h]
        send(("far_a", k, h), part.at[k, across, :, pl.ds(lo, n)], far_a.at[k, h, :, pl.ds(0, n)],
             far_as, (k, h), xpeers[h])
        d = 1 - h
        send(("fin_a", k, d), part.at[k, (right, left)[d], :, pl.ds(lo, n)],
             fin_a.at[k, d, :, pl.ds(0, n)], fin_as, (k, d), xpeers[d])

    def ready(k, which):
        wait(("c", 1 if which == 2 else 0, k))
        wait(("w", which))
        if which not in seen:
            seen.add(which)
            loads[which].wait()

    def forward_a(k):
        for which in range(2):
            ready(k, which)
            product(k, which, 0, NA)
        send_a(k, 0)

    def forward_h(k):
        ready(k, 2)
        product(k, 2, 0, NA)
        send_a(k, 1)

    def middle_a(k):
        for d in range(2):
            lo, n = halves(ga, k)[d]
            wait(("far_a", k, d))
            value = full[k, (right, left)[d], :, lo : lo + n] + far_a[k, d, :, :n].astype(F32)
            mid_a[k, d, :, :n] = value.astype(BF16)
            span = pl.ds(0, n)
            send(("sum_a", k, d), mid_a.at[k, d, :, span], sum_a.at[k, d, :, span],
                 sum_as, (k, d), xpeers[d])

    def second_a(k):
        for d in range(2):
            wait(("fin_a", k, d))
        for d in range(2):
            wait(("sum_a", k, d))
        for zz in (1 - z, z):
            for d in range(2):
                lo, n = halves(ga, k)[d]
                value = (full[k, x, zz, lo : lo + n] + sum_a[k, d, zz, :n].astype(F32)
                         + fin_a[k, 1 - d, zz, :n].astype(F32))
                if zz is z:
                    own_a[k, lo : lo + n] = value
                else:
                    out_a[k, lo : lo + n] = value.astype(BF16)
            if zz is not z:
                send(("z_a", k), out_a.at[k], in_a.at[k], z_as, (k,), zpeer)

    def point_a(k):
        wait(("z_a", k))
        value = own_a[k] + in_a[k].astype(F32)
        results = pointwise(value[:NA], value[NA : 2 * NA], value[2 * NA :])
        for which in range(3):
            hb[k, x, z, which * NA : (which + 1) * NA] = results[which]
        block = hb.at[k, x, z, pl.ds(0, ga)]
        send(("gz_a", k), block, block, gz_as, (k,), zpeer)
        along_x(k, block, 0)

    def along_x(k, block, part_of):
        for d in range(2):
            send(("gx_a", k, d, part_of), block, block, gx_as, (k, d, part_of), xpeers[d])
        if k == DIRECT:
            send(("gw_a", k, part_of), block, block, gw_as, (k, part_of), apeer)

    def across_a(k):
        wait(("gz_a", k))
        along_x(k, hb.at[k, x, 1 - z, pl.ds(0, ga)], 1)

    def onward_a(k):
        for d in range(2):
            lo, n = halves(ga, k)[d]
            for part_of in range(2):
                wait(("gx_a", k, d, part_of))
            block = hb.at[k, (left, right)[d], :, pl.ds(lo, n)]
            send(("gw_a", k, d), block, block, gw_as, (k, d), xpeers[d])

    def share_a(k):
        for d in range(2):
            for part_of in range(2):
                wait(("gx_a", k, d, part_of))
            wait(("gw_a", k, d))
        send(("sh_a", k), hb.at[k, :, :, pl.ds(0, ga)], hs.at[k, :, :, pl.ds(0, ga)], sh_as, (k,), speer)

    def forward_b(k):
        for which in range(3):
            ready(k, which)
            product(k, which, NA, nb)
        send(("z_b", k), part.at[k, :, 1 - z, pl.ds(ga, gb)], in_b.at[k], z_bs, (k,), zpeer)

    def second_b(k):
        wait(("z_b", k))
        value = full[k, :, z, ga:] + in_b[k].astype(F32)
        full_b[k] = value
        part_b[k] = value.astype(BF16)
        for d in range(2):
            lo, n = halves(gb, k)[d]
            send(("far_b", k, d), part_b.at[k, across, pl.ds(lo, n)], far_b.at[k, d, pl.ds(0, n)],
                 far_bs, (k, d), xpeers[d])
        for d in range(2):
            lo, n = halves(gb, k)[1 - d]
            send(("fin_b", k, d), part_b.at[k, (right, left)[d], pl.ds(lo, n)],
                 fin_b.at[k, d, pl.ds(0, n)], fin_bs, (k, d), xpeers[d])

    def middle_b(k):
        for d in range(2):
            lo, n = halves(gb, k)[d]
            wait(("far_b", k, d))
            value = full_b[k, (right, left)[d], lo : lo + n] + far_b[k, d, :n].astype(F32)
            mid_b[k, d, :n] = value.astype(BF16)
            span = pl.ds(0, n)
            send(("sum_b", k, d), mid_b.at[k, d, span], sum_b.at[k, d, span], sum_bs, (k, d), xpeers[d])

    def point_b(k):
        for d in range(2):
            wait(("fin_b", k, d))
        for d in range(2):
            wait(("sum_b", k, d))
        for d in range(2):
            lo, n = halves(gb, k)[d]
            tot[lo : lo + n] = (full_b[k, x, lo : lo + n] + sum_b[k, d, :n].astype(F32)
                                + fin_b[k, 1 - d, :n].astype(F32))
        results = pointwise(tot[:nb], tot[nb : 2 * nb], tot[2 * nb :])
        for which in range(3):
            hb[k, x, z, ga + which * nb : ga + (which + 1) * nb] = results[which]
        block = hb.at[k, x, z, pl.ds(ga, gb)]
        for d in range(2):
            send(("gx_b", k, d), block, block, gx_bs, (k, d), xpeers[d])
        send(("gz_b", k, 0), block, block, gz_bs, (k, 0), zpeer)
        if k == DIRECT:
            send(("gw_b", k, 0), block, block, gw_bs, (k, 0), apeer)

    def onward_b(k):
        for d in range(2):
            wait(("gx_b", k, d))
            if k != DIRECT:
                lo, n = halves(gb, k)[d]
                block = hb.at[k, (left, right)[d], z, pl.ds(ga + lo, n)]
                send(("gw_b", k, d), block, block, gw_bs, (k, d), xpeers[d])
        for d in range(2):
            block = hb.at[k, (left, right)[d], z, pl.ds(ga, gb)]
            send(("gz_b", k, 1 + d), block, block, gz_bs, (k, 1 + d), zpeer)

    def across_b(k):
        for d in range(1 if k == DIRECT else 2):
            wait(("gw_b", k, d))
        block = hb.at[k, across, z, pl.ds(ga, gb)]
        send(("gz_b", k, 3), block, block, gz_bs, (k, 3), zpeer)

    def share_b(k):
        for i in range(4):
            wait(("gz_b", k, i))
        send(("sh_b", k), hb.at[k, :, :, pl.ds(ga, gb)], hs.at[k, :, :, pl.ds(ga, gb)], sh_bs, (k,), speer)

    def flat(ref, k, first, n):
        return [ref[k, :, :, first + g].reshape(NX * NZ * 16, 128) for g in range(n)]

    def back(k, base, lo, n):
        dg = jnp.concatenate(flat(hb, k, base + n, n), axis=1)
        du = jnp.concatenate(flat(hb, k, base + 2 * n, n), axis=1)
        span = pl.ds(lo * 128, n * 128)
        again = k in begun
        begun.add(k)
        for h, ref in ((sib, gq), (c, gp)):
            value = contract_last(dg, wg[h, :, span]) + contract_last(du, wu[h, :, span])
            ref[k] = ref[k] + value if again else value
            if again and ref is gq:
                send(("p", k), gq.at[k], gr.at[k], psem, (k,), speer)

    def back_a(k):
        back(k, 0, 0, NA)

    def back_b(k):
        back(k, ga, NA, nb)

    def cols_send(k):
        wait(("p", k))
        gp[k] = gp[k] + gr[k]
        for i in (2, 1, 3):
            sd[k, i - 1] = gp[k, yrows(i), :].astype(BF16)
            send(("d", k, i), sd.at[k, i - 1], rd.at[k, i - 1], dsem, (k, i - 1), ypeer(i))

    def cols_sum(k):
        value = gp[k, yrows(0), :]
        for i in (1, 3, 2):
            wait(("d", k, i))
            value = value + rd[k, i - 1].astype(F32)
        i = ORDER[k]
        if i == 0:
            own_t[...] = value
        else:
            se[i - 1] = value.astype(BF16)
            send(("e", i), se.at[i - 1], re.at[i - 1], esem, (i - 1,), hpeer(i))

    def finish(_):
        value = own_t[...]
        for i in (1, 3, 2):
            wait(("e", i))
            value = value + re[i - 1].astype(F32)
        gtok_ref[...] = value.astype(BF16)

    def weight_grads(n):
        ref, half = (hb, c) if n < 3 else (hs, sib)
        which = (1, 2, 0)[n % 3]
        if n >= 3:
            for k in range(CHUNKS):
                wait(("sh_a", k))
                wait(("sh_b", k))
        cols = [jnp.concatenate(v, axis=0) for v in zip(*(
            flat(ref, k, which * NA, NA) + flat(ref, k, ga + which * nb, nb) for k in range(CHUNKS)))]
        units = jnp.concatenate(cols, axis=1)
        acted = jnp.concatenate([acts[c, plane(k), 1 if which == 0 else 0] for k in range(CHUNKS)], axis=0)
        span = pl.ds(pl.multiple_of(half * width, 128), width)
        if which == 0:
            od[span, :] = contract_first(units, acted).astype(BF16)
        else:
            (og, ou)[which - 1][:, span] = contract_first(acted, units).astype(BF16)

    stages = dict(
        Z=pass_y, V=pass_weighted, T=take, U=take_weighted, FA=forward_a, FH=forward_h, FB=forward_b, MA=middle_a, SA=second_a, PA=point_a, AA=across_a,
        WA=onward_a, HA=share_a, SB=second_b, MB=middle_b, PB=point_b, WB=onward_b, YB=across_b,
        HB=share_b, BA=back_a, BB=back_b, C=cols_send, D=cols_sum, E=finish, G=weight_grads)
    for item in SCHEDULE:
        for copy in sent[:4]:
            if len(sent) > 30:
                sent.remove(copy)
                copy.wait_send()
        stages[item[:-1]](int(item[-1]))
    for copy in sent:
        copy.wait_send()


def write_kernel(*refs):
    n = len(refs) // 2
    sem = refs[-1]
    copies = [pltpu.make_async_copy(refs[i], refs[n + i], sem.at[i]) for i in range(n)]
    for copy in copies:
        copy.start()
    for copy in copies:
        copy.wait()


def local(tokens, out_grad, seq_ids, confidence, gate_weight, up_weight, down_weight):
    rows, depth = tokens.shape
    width = gate_weight.shape[1] // 2
    groups = width // 128
    nb = groups - NA
    ga, gb = 3 * NA, 3 * nb
    ha, hb = (ga + 1) // 2, (gb + 1) // 2
    total = ga + gb
    chunk = rows * NY
    k = CHUNKS
    vm, sm, dma = pltpu.VMEM, pltpu.SMEM, pltpu.SemaphoreType.DMA
    anyspace = pl.BlockSpec(memory_space=pl.ANY)
    vmspace = pl.BlockSpec(memory_space=pltpu.VMEM)
    one, two = dma((2, k)), dma((2, k, 2))
    shapes = (rows, depth), (depth, 2 * width), (depth, 2 * width), (2 * width, depth)
    results = pl.pallas_call(
        main_kernel,
        name="exchange",
        out_shape=tuple(vm(shape, BF16) for shape in shapes),
        in_specs=[anyspace] * 7,
        out_specs=(vmspace,) * 4,
        scratch_shapes=[
            sm(seq_ids.shape, jnp.int32),
            sm(confidence.shape, jnp.int32),
            vm((rows, depth), BF16),
            vm((2, NH, 2, chunk, depth), BF16),
            vm((2, depth, width), BF16),
            vm((2, depth, width), BF16),
            vm((2, width, depth), BF16),
            vm((k, NX, NZ, total, 16, 128), BF16),
            vm((k, NX, NZ, total, 16, 128), F32),
            vm((k, 2, NZ, ha, 16, 128), BF16),
            vm((k, 2, NZ, ha, 16, 128), BF16),
            vm((k, 2, NZ, ha, 16, 128), BF16),
            vm((k, 2, NZ, ha, 16, 128), BF16),
            vm((k, ga, 16, 128), BF16),
            vm((k, ga, 16, 128), BF16),
            vm((k, ga, 16, 128), F32),
            vm((k, NX, gb, 16, 128), BF16),
            vm((k, NX, gb, 16, 128), F32),
            vm((k, NX, gb, 16, 128), BF16),
            vm((k, 2, hb, 16, 128), BF16),
            vm((k, 2, hb, 16, 128), BF16),
            vm((k, 2, hb, 16, 128), BF16),
            vm((k, 2, hb, 16, 128), BF16),
            vm((gb, 16, 128), F32),
            vm((k, NX, NZ, total, 16, 128), BF16),
            vm((k, NX, NZ, total, 16, 128), BF16),
            vm((k, chunk, depth), F32),
            vm((k, chunk, depth), F32),
            vm((k, chunk, depth), F32),
            vm((k, 3, rows, depth), BF16),
            vm((k, 3, rows, depth), BF16),
            vm((3, rows, depth), BF16),
            vm((3, rows, depth), BF16),
            vm((rows, depth), F32),
            dma((7,)), dma((2, 3)), dma((2, 2, 3)), dma((2, 2, k, 3)), dma((2, 2, k)),
            two, two, two, one, one, dma((2, k, 2, 2)), two, one,
            two, two, two, one, dma((2, k, 4)), two, two, one,
            one, dma((2, k, 3)), dma((2, 3)),
        ],
        compiler_params=pltpu.CompilerParams(
            collective_id=0, has_side_effects=True, vmem_limit_bytes=48 << 20),
    )(*(pltpu.with_memory_space_constraint(v, pltpu.HBM) for v in (
        seq_ids, confidence, tokens, out_grad, gate_weight, up_weight, down_weight)))
    return pl.pallas_call(
        write_kernel,
        name="write_out",
        out_shape=tuple(jax.ShapeDtypeStruct(shape, BF16) for shape in shapes),
        in_specs=[vmspace] * 4,
        out_specs=(anyspace,) * 4,
        scratch_shapes=[dma((4,))],
        compiler_params=pltpu.CompilerParams(vmem_limit_bytes=16 << 20),
    )(*(pltpu.with_memory_space_constraint(v, pltpu.VMEM) for v in results))


def solution(mesh):
    placed = (
        P("col", "row"),
        P("col", "row"),
        P("col"),
        P(),
        P("row", "col"),
        P("row", "col"),
        P("col", "row"),
    )
    return jax.shard_map(
        local,
        mesh=mesh,
        in_specs=placed,
        out_specs=(P("col", "row"), P("row", "col"), P("row", "col"), P("col", "row")),
        check_vma=False,
    )
```
